32 devices in a mesh: dom: 8 (over z, x), sub: 4 (over y, core).
Axes of the slice: x: 2, y: 2, z: 4, core: 2. Of those that a mesh axis runs over, the one named last changes fastest.
Arguments:
- features: bfloat16 [8192, 2048], P(('dom', 'sub')), may hold values from -30 to 30
- weight: bfloat16 [2048, 2048], replicated, may hold values from -0.125 to 0.125
- bn_gain: float32 [2048], replicated, may hold values from 0.5 to 2
- bn_shift: float32 [2048], replicated, may hold values from -1 to 1
- cotangent: bfloat16 [8192, 2048], P(('dom', 'sub')), may hold values from -6 to 6
- neighbours: int32 [8192, 50], P(('dom', 'sub')), may hold values from 0 to 511, as said below
- degrees: int32 [8192], P(('dom', 'sub')), may hold values from 1 to 50
- send_rows: int32 [32, 8, 4, 8], P(('dom', 'sub')), may hold values from 0 to 255
- valid_nodes: int32 [8192], P(('dom', 'sub')), may hold values 0 or 1
Outputs:
- activations: bfloat16 [8192, 2048], P(('dom', 'sub'))
- grad_features: float32 [8192, 2048], P(('dom', 'sub'))
- grad_weight: float32 [2048, 2048], P('sub')
- grad_gain: float32 [2048], replicated
- grad_shift: float32 [2048], replicated
The draws below stay inside these ranges and needn't reach their ends.
Inputs may be any that keep to these rules, and one draw needn't show every extreme that they name: `neighbours`: an entry below 256 is a row of the node's own device; an entry 256 + p * 8 + q is slot q of what device p sends to this device, and such entries name only slots that p fills (from one device to another 1 to 8 slots are filled, differing from pair to pair; some pair fills all 8). Entries at positions at or past the node's degree may be any value in range.
All inputs are finite; a program needn't handle non-finite values. No bound on the sum of `valid_nodes` on one device may be relied on, other than what follows from the above.
Results may differ from the reference program's by a relative error of at most 0.0091.
Values may be sent and summed in bfloat16 or wider, within the bound.
No kernel may reach another device: no remote copies, remote signals or barrier semaphores. Data moves between devices by JAX's collectives and lax.ppermute only.
A program may use at most 192 MiB of HBM per device.

```python
import math
import jax
import jax.numpy as jnp
from jax import lax

F = 2048
DEG = 50
SLOT = 8
NODE_DEV = 256
NODES = 8192
N_DOM = 8
N_SUB = 4
DEVICES = 32


def halo_counts(key):
    key = jax.random.fold_in(key, 11)
    first, second = jax.random.split(key)
    counts = jax.random.randint(first, (DEVICES, DEVICES), 1, SLOT + 1)
    offset = jax.random.randint(second, (), 0, DEVICES)
    source = (jnp.arange(DEVICES) + offset) % DEVICES
    filled = source[None, :] == jnp.arange(DEVICES)[:, None]
    return (jnp.where(filled, SLOT, counts), offset)


def draw_neighbours(key, part):
    counts, offset = halo_counts(key)
    key = jax.random.fold_in(key, 5)
    key_local, key_source, key_slot, key_remote = jax.random.split(key, 4)
    draw_shape = (NODES, DEG)
    device_of = (jnp.arange(NODES) // NODE_DEV)[:, None]
    local_row = jax.random.randint(key_local, draw_shape, 0, NODE_DEV)
    source = jax.random.randint(key_source, draw_shape, 0, DEVICES)
    slot_index = jax.random.randint(key_slot, draw_shape, 0, SLOT)
    usable = slot_index < counts[source, device_of]
    remote = jax.random.randint(key_remote, draw_shape, 0, 4) == 0
    halo_entry = NODE_DEV + source * SLOT + slot_index
    result = jnp.where(remote & usable, halo_entry, local_row)
    target = (DEVICES - 1 - offset) % DEVICES
    result = result.at[target * NODE_DEV, 0].set(NODE_DEV + DEVICES * SLOT - 1)
    result = result.at[0, 1].set(0)
    return result.astype(jnp.int32)


def draw_features(key, part):
    key = jax.random.fold_in(key, 7)
    key_scale, key_value = jax.random.split(key, 2)
    rising = 0.5 + (jnp.arange(NODES) // NODE_DEV).astype(jnp.float32) / (DEVICES - 1)
    roughness = jnp.exp(jax.random.uniform(key_scale, (NODES, 1), minval=-1.15, maxval=1.15))
    values = jnp.clip(jax.random.normal(key_value, (NODES, F)), -5.0, 5.0)
    return (values * roughness * rising[:, None]).astype(jnp.bfloat16)


def place_ends(entries, own_key, smallest, top_value):
    shape = entries.shape
    index_at = [jax.random.randint(jax.random.fold_in(own_key, axis), (), 0, shape[axis]) for axis in range(len(shape))]
    entries = entries.at[tuple(index_at)].set(smallest)
    longest = shape.index(max(shape))
    index_at[longest] = (index_at[longest] + 1) % shape[longest]
    return entries.at[tuple(index_at)].set(top_value)


def levels(own_key, dims, shards, low, top_value):
    def one(dim, shards_of):
        heights = jax.random.uniform(jax.random.fold_in(jax.random.fold_in(own_key, 6), dim), (shards_of,), jnp.float32, low / len(shards), top_value / len(shards))
        return jnp.repeat(jnp.exp(heights), dims[dim] // shards_of).reshape((-1,) + (1,) * (len(dims) - dim - 1))

    gain = one(*shards[0])
    for cut in shards[1:]:
        gain = gain * one(*cut)
    return gain


def gaussian(rng, dims, width, limit, pieces=(), kind=jnp.bfloat16):
    loudness = levels(rng, dims, pieces, -0.22, 0.18) if pieces else 1.0
    drawn = jax.random.normal(rng, dims, jnp.float32) * width * loudness
    return jnp.minimum(jnp.maximum(drawn, -limit), limit).astype(kind)


def setup_inputs(seed: int = 0) -> dict:
    key_list = jax.random.split(jax.random.key(seed), 10)
    features = draw_features(jax.random.fold_in(key_list[9], 71), 0)
    weight = gaussian(key_list[1], (F, F), F ** -0.5, 0.125)
    bn_gain = jnp.clip(jnp.exp(jax.random.uniform(key_list[2], (F,), jnp.float32, math.log(0.5), math.log(2.0))), 0.5, 2.0)
    bn_shift = jnp.clip(jax.random.uniform(key_list[3], (F,), jnp.float32, -1.0, 1.0), -1.0, 1.0)
    cotangent = gaussian(key_list[4], (NODES, F), 1.0, 6.0, ((0, 32),))
    neighbours = draw_neighbours(jax.random.fold_in(key_list[9], 71), 0)
    degrees = place_ends(jax.random.randint(key_list[6], (NODES,), 1, DEG + 1), jax.random.fold_in(key_list[6], 1), 1, DEG).astype(jnp.int32)
    send_rows = place_ends(jax.random.randint(key_list[7], (DEVICES, N_DOM, N_SUB, SLOT), 0, NODE_DEV), jax.random.fold_in(key_list[7], 1), 0, NODE_DEV - 1).astype(jnp.int32)
    valid_nodes = place_ends((jax.random.randint(key_list[8], (NODES,), 0, 8) < 7).astype(jnp.int32), jax.random.fold_in(key_list[8], 1), 0, 1)
    return dict(features=features, weight=weight, bn_gain=bn_gain, bn_shift=bn_shift, cotangent=cotangent, neighbours=neighbours, degrees=degrees, send_rows=send_rows, valid_nodes=valid_nodes)


epsilon = 1e-05

@jax.custom_vjp
def low(v):
    return lax.optimization_barrier(v.astype(jnp.bfloat16)).astype(jnp.float32)

@jax.custom_vjp
def low_back(v):
    return v

def low_keep(v):
    return (low(v), None)

def low_pass(kept, grad):
    return (grad,)

def back_keep(v):
    return (v, None)

def back_low(kept, grad):
    return (low(grad),)
low.defvjp(low_keep, low_pass)
low_back.defvjp(back_keep, back_low)

def global_index(neighbours, send_rows):
    node_count = neighbours.shape[0]
    device_of = jnp.arange(node_count, dtype=jnp.int32) // NODE_DEV
    dom_index = device_of // N_SUB
    sub_index = device_of % N_SUB
    halo_offset = jnp.maximum(neighbours - NODE_DEV, 0)
    source = (halo_offset // SLOT).astype(jnp.int32)
    slot_index = (halo_offset % SLOT).astype(jnp.int32)
    sent_row = send_rows[source, dom_index[:, None], sub_index[:, None], slot_index]
    remote = source * NODE_DEV + sent_row
    local_row = device_of[:, None] * NODE_DEV + neighbours
    return jnp.where(neighbours < NODE_DEV, local_row, remote).astype(jnp.int32)

def reference(features, weight, bn_gain, bn_shift, cotangent, neighbours, degrees, send_rows, valid_nodes):
    node_count, feat_width = features.shape
    lookup = global_index(neighbours, send_rows)
    nbr_taken = (jnp.arange(DEG, dtype=jnp.int32)[None, :] < degrees[:, None]).astype(jnp.float32)
    degree_scale = 1.0 / (degrees.astype(jnp.float32) + 1.0)
    node_mask = valid_nodes.astype(jnp.float32)[:, None]
    block_rows = math.gcd(node_count, 256)
    count_blocks = node_count // block_rows

    def forward(feat_f, weight_f, gain_f, shift_f):
        low_features = low(feat_f)

        def aggregate(block_args):
            nbr_index, chosen, factor, own_rows = block_args
            gathered = low_features[nbr_index]
            summed_rows = jnp.einsum('rk,rkf->rf', chosen, gathered, precision=lax.Precision.HIGHEST)
            return (summed_rows + 2.0 * own_rows) * factor[:, None]
        aggregated = lax.map(jax.checkpoint(aggregate), (lookup.reshape(count_blocks, block_rows, DEG), nbr_taken.reshape(count_blocks, block_rows, DEG), degree_scale.reshape(count_blocks, block_rows), low_features.reshape(count_blocks, block_rows, feat_width))).reshape(node_count, feat_width)
        linear = low_back(jnp.dot(low(aggregated), weight_f, precision=lax.Precision.HIGHEST))
        valid_count = jnp.sum(node_mask)
        column_mean = lax.optimization_barrier(jnp.sum(node_mask * linear, 0)) / valid_count
        centred = linear - column_mean
        variance = lax.optimization_barrier(jnp.sum(node_mask * centred * centred, 0)) / valid_count
        normed = centred * lax.rsqrt(variance + epsilon)
        return node_mask * jax.nn.gelu(gain_f * normed + shift_f)
    output, pullback = jax.vjp(forward, features.astype(jnp.float32), weight.astype(jnp.float32), bn_gain, bn_shift)
    grad_features, grad_weight, grad_gain, grad_shift = pullback(cotangent.astype(jnp.float32))
    return (output.astype(jnp.bfloat16), grad_features, grad_weight, grad_gain, grad_shift)
```

```python
import jax
import jax.numpy as jnp
from jax import lax
from jax.sharding import PartitionSpec as P

epsilon = 1e-05
both_axes = ("dom", "sub")
contract_rows = (((0,), (0,)), ((), ()))


def swap(value, axis, offset):
    size = lax.axis_size(axis)
    return lax.ppermute(value, axis, [(i, i ^ offset) for i in range(size)])


def tree_sum(terms):
    while len(terms) > 1:
        terms = [terms[i] + terms[i + 1] for i in range(0, len(terms), 2)]
    return terms[0]


def exchange_steps():
    steps = []
    for axis in ("sub", "dom"):
        size, low = lax.axis_size(axis), 1
        odd = (size.bit_length() - 1) % 2
        while low < size:
            width = 2 if odd else 4
            odd = 0
            steps.append((axis, [low * k for k in range(1, width)]))
            low *= width
    return steps


def sum_over_all(value):
    for axis, offsets in exchange_steps():
        value = tree_sum([value] + [swap(value, axis, offset) for offset in offsets])
    return value


def merge_statistics(count, total, squares):
    packed = jnp.stack([jnp.broadcast_to(count, total.shape), total, squares])
    for axis, offsets in exchange_steps():
        parts = [packed] + [swap(packed, axis, offset) for offset in offsets]
        count = tree_sum([p[0] for p in parts])
        total = tree_sum([p[1] for p in parts])
        mean = total / jnp.maximum(count, 1.0)
        squares = tree_sum(
            [p[2] + p[0] * jnp.square(p[1] / jnp.maximum(p[0], 1.0) - mean) for p in parts]
        )
        packed = jnp.stack([count, total, squares])
    return packed[0], packed[1], packed[2]


def half(value, axis, which):
    size = value.shape[axis] // 2
    return lax.dynamic_slice_in_dim(value, which * size, size, axis)


def join(own, received, axis, bit):
    return jnp.where(
        bit == 0,
        jnp.concatenate([own, received], axis),
        jnp.concatenate([received, own], axis),
    )


def rounded(value):
    return lax.reduce_precision(value, 8, 7).astype(jnp.bfloat16)


def weight_gradient(mixed_rows, grad_linear):
    sub, dom = lax.axis_index("sub"), lax.axis_index("dom")
    core, line = sub & 1, sub >> 1
    mixed_own = half(mixed_rows, 1, line)
    mixed_line = swap(half(mixed_rows, 1, 1 - line), "sub", 2)
    mixed_core = swap(jnp.concatenate([mixed_own, mixed_line]), "sub", 1)
    rows = mixed_rows.shape[0]
    grad_own = half(grad_linear, 1, core)
    grad_core = swap(half(grad_linear, 1, 1 - core), "sub", 1)
    grad_pair = jnp.concatenate([grad_own, grad_core])
    grad_far = swap(grad_pair, "sub", 2)
    part = lax.dot_general(
        jnp.concatenate([mixed_own, mixed_core[:rows]]),
        grad_pair,
        contract_rows,
        preferred_element_type=jnp.float32,
    ) + lax.dot_general(
        jnp.concatenate([mixed_line, mixed_core[rows:]]),
        grad_far,
        contract_rows,
        preferred_element_type=jnp.float32,
    )
    bits = [1 << k for k in range(lax.axis_size("dom").bit_length() - 1)]
    dims = [1] + [0] * (len(bits) - 1)
    for bit, dim in zip(bits, dims):
        mine = (dom & bit) // bit
        part = half(part, dim, mine) + swap(
            rounded(half(part, dim, 1 - mine)), "dom", bit
        ).astype(jnp.float32)
    part = rounded(part)
    for bit, dim in zip(bits[::-1], dims[::-1]):
        mine = (dom & bit) // bit
        part = join(part, swap(part, "dom", bit), dim, mine)
    other = swap(half(part, 0, 1 - core), "sub", 1)
    return join(half(part, 0, core), other, 1, core).astype(jnp.float32)


def on_device(
    features, weight, bn_gain, bn_shift, cotangent, neighbours, degrees, send_rows, valid_nodes
):
    node_rows, feat_width = features.shape
    routes = send_rows.reshape(-1)
    halo_rows = routes.shape[0]
    devices = lax.axis_size("dom") * lax.axis_size("sub")

    def to_all(rows):
        rows = rows.reshape(devices, halo_rows // devices, feat_width)
        return lax.all_to_all(rows, both_axes, 0, 0, tiled=True).reshape(halo_rows, feat_width)

    pick = (
        routes[:, None] == lax.broadcasted_iota(jnp.int32, (halo_rows, node_rows), 1)
    ).astype(jnp.bfloat16)
    outgoing = jnp.dot(pick, features, preferred_element_type=jnp.float32).astype(jnp.bfloat16)
    arrived = to_all(outgoing)
    node_mask = valid_nodes.astype(jnp.float32)[:, None]
    degree_scale = 1.0 / (degrees.astype(jnp.float32) + 1.0)
    nbr_taken = lax.broadcasted_iota(jnp.int32, neighbours.shape, 1) < degrees[:, None]
    table_rows = node_rows + halo_rows
    table_iota = lax.broadcasted_iota(jnp.int32, (1, 1, table_rows), 2)
    matches = (neighbours[:, :, None] == table_iota) & nbr_taken[:, :, None]
    counts = jnp.sum(matches.astype(jnp.float32), 1)
    own_counts = (counts[:, :node_rows] + 2.0 * jnp.eye(node_rows, dtype=jnp.float32)).astype(
        jnp.bfloat16
    )
    halo_counts = counts[:, node_rows:].astype(jnp.bfloat16)
    summed = jnp.dot(own_counts, features, preferred_element_type=jnp.float32) + jnp.dot(
        halo_counts, arrived, preferred_element_type=jnp.float32
    )
    mixed_rows = (summed * degree_scale[:, None]).astype(jnp.bfloat16)
    linear = jnp.dot(mixed_rows, weight, preferred_element_type=jnp.float32)
    own_count = jnp.sum(node_mask)
    own_total = jnp.sum(node_mask * linear, 0)
    own_centred = linear - own_total / jnp.maximum(own_count, 1.0)
    valid_count, column_total, spread = merge_statistics(
        own_count, own_total, jnp.sum(node_mask * own_centred * own_centred, 0)
    )
    column_mean = column_total / valid_count
    centred = linear - column_mean
    variance = spread / valid_count
    inverse = lax.rsqrt(variance + epsilon)
    normed = centred * inverse
    shifted = bn_gain * normed + bn_shift
    active, gelu_back = jax.vjp(jax.nn.gelu, shifted)
    activations = (node_mask * active).astype(jnp.bfloat16)
    (gelu_slope,) = gelu_back(cotangent.astype(jnp.float32) * node_mask)
    grad_gain, grad_shift = sum_over_all(
        jnp.stack([jnp.sum(gelu_slope * normed, 0), jnp.sum(gelu_slope, 0)])
    )
    grad_linear = (
        node_mask
        * bn_gain
        * inverse
        * (gelu_slope - (grad_shift + normed * grad_gain) / valid_count)
    ).astype(jnp.bfloat16)
    grad_mixed = lax.dot_general(
        grad_linear, weight, (((1,), (1,)), ((), ())), preferred_element_type=jnp.float32
    )
    weighted = (grad_mixed * degree_scale[:, None]).astype(jnp.bfloat16)
    halo_grad = lax.dot_general(
        halo_counts, weighted, contract_rows, preferred_element_type=jnp.float32
    ).astype(jnp.bfloat16)
    returned = to_all(halo_grad)
    grad_weight = weight_gradient(mixed_rows, grad_linear)
    grad_features = lax.dot_general(
        own_counts, weighted, contract_rows, preferred_element_type=jnp.float32
    ) + lax.dot_general(pick, returned, contract_rows, preferred_element_type=jnp.float32)
    return (activations, grad_features, grad_weight, grad_gain, grad_shift)


def solution(mesh):
    return jax.shard_map(
        on_device,
        mesh=mesh,
        in_specs=(
            P(("dom", "sub"), None),
            P(),
            P(),
            P(),
            P(("dom", "sub"), None),
            P(("dom", "sub"), None),
            P(("dom", "sub")),
            P(("dom", "sub"), None, None, None),
            P(("dom", "sub")),
        ),
        out_specs=(P(("dom", "sub"), None), P(("dom", "sub"), None), P("sub", None), P(), P()),
        check_vma=False,
    )
```

```python
import functools

import jax
import jax.numpy as jnp
from jax import lax
from jax.experimental import pallas as pl
from jax.experimental.pallas import tpu as pltpu
from jax.sharding import PartitionSpec as P

epsilon = 1e-05
both_axes = ("dom", "sub")
contract_rows = (((0,), (0,)), ((), ()))
contract_columns = (((1,), (1,)), ((), ()))
tile = 256
splits = 1
vmem_bytes = 50 * 2**20


def swap(value, axis, offset):
    size = lax.axis_size(axis)
    return lax.ppermute(value, axis, [(i, i ^ offset) for i in range(size)])


def tree_sum(terms):
    while len(terms) > 1:
        terms = [terms[i] + terms[i + 1] for i in range(0, len(terms), 2)]
    return terms[0]


def exchange_steps():
    steps = []
    for axis in ("sub", "dom"):
        size, low = lax.axis_size(axis), 1
        odd = (size.bit_length() - 1) % 2
        while low < size:
            width = 2 if odd else 4
            odd = 0
            steps.append((axis, [low * k for k in range(1, width)]))
            low *= width
    return steps


def sum_over_all(value):
    for axis, offsets in exchange_steps():
        value = tree_sum([value] + [swap(value, axis, offset) for offset in offsets])
    return value


def merge_statistics(packed):
    steps = []
    for axis, offsets in exchange_steps():
        parts = [packed] + [swap(packed, axis, offset) for offset in offsets]
        count = tree_sum([p[0] for p in parts])
        total = tree_sum([p[1] for p in parts])
        mean = total / jnp.maximum(count, 1.0)
        squares = tree_sum(
            [p[2] + p[0] * jnp.square(p[1] / jnp.maximum(p[0], 1.0) - mean) for p in parts]
        )
        packed = jnp.stack([count, total, squares])
        steps.append(packed)
    return packed, steps


def after(value, *others):
    return lax.optimization_barrier((value,) + others)[0]


def half(value, axis, which):
    size = value.shape[axis] // 2
    return lax.dynamic_slice_in_dim(value, which * size, size, axis)


def join(own, received, axis, bit):
    return jnp.where(
        bit == 0,
        jnp.concatenate([own, received], axis),
        jnp.concatenate([received, own], axis),
    )


def rounded(value):
    return lax.reduce_precision(value, 8, 7).astype(jnp.bfloat16)


def call(kernel, grid, in_specs, out_specs, out_shape, flops, scratch=(), prefetch=0):
    return pl.pallas_call(
        kernel,
        grid_spec=pltpu.PrefetchScalarGridSpec(
            num_scalar_prefetch=prefetch,
            grid=grid,
            in_specs=in_specs,
            out_specs=out_specs,
            scratch_shapes=scratch,
        ),
        out_shape=out_shape,
        compiler_params=pltpu.CompilerParams(
            dimension_semantics=("arbitrary",) * len(grid), vmem_limit_bytes=vmem_bytes
        ),
        cost_estimate=pl.CostEstimate(flops=flops, bytes_accessed=4 * 2**20, transcendentals=0),
    )


def whole(shape):
    return pl.BlockSpec(shape, lambda *_: (0,) * len(shape))


def columns(rows, width=tile):
    return pl.BlockSpec((rows, width), lambda i, *_: (0, i))


def blocks(rows, width):
    return pl.BlockSpec((1, rows, width), lambda i, *_: (i, 0, 0))


def struct(shape, dtype=jnp.float32):
    return jax.ShapeDtypeStruct(shape, dtype)


def dot(a, b, dims=(((1,), (0,)), ((), ()))):
    return lax.dot_general(a, b, dims, preferred_element_type=jnp.float32)


def linear_kernel(
    counts, features, arrived, scale, mask, weight, mixed_out, linear_out, stats_out, mixed
):
    rows, width = features.shape
    piece = mixed_out.shape[2]

    @pl.when(pl.program_id(0) == 0)
    def _():
        for j in range(width // piece):
            part = slice(j * piece, (j + 1) * piece)
            summed = dot(counts[:, :rows], features[:, part]) + dot(
                counts[:, rows:], arrived[:, part]
            )
            value = (summed * scale[...]).astype(jnp.bfloat16)
            mixed[:, part] = value
            mixed_out[j] = value

    linear = dot(mixed[...], weight[...])
    linear_out[...] = linear
    count = jnp.sum(mask[...])
    total = jnp.sum(mask[...] * linear, 0, keepdims=True)
    off = linear - total / jnp.maximum(count, 1.0)
    squares = jnp.sum(mask[...] * off * off, 0, keepdims=True)
    stats_out[...] = jnp.concatenate([jnp.full_like(total, count), total, squares], 0)


def normalise(linear, stats):
    count = stats[0:1, :]
    inverse = lax.rsqrt(stats[2:3, :] / count + epsilon)
    return (linear - stats[1:2, :] / count) * inverse, inverse, count


def gelu_kernel(
    linear, stats, gain, shift, cotangent, mask, active_out, slope_out, sums_out
):
    normed, _, _ = normalise(linear[...], stats)
    value = gain[...] * normed + shift[...]
    root, cubic = 0.7978845608028654, 0.044715
    square = value * value
    bent = jnp.tanh(root * value * (1.0 + cubic * square))
    upper = 0.5 * (1.0 + bent)
    active_out[...] = (mask[...] * (value * upper)).astype(jnp.bfloat16)
    inner = 0.5 * root * value * (1.0 - bent * bent) * (1.0 + 3.0 * cubic * square)
    slope = mask[...] * cotangent[...].astype(jnp.float32) * (upper + inner)
    slope_out[...] = slope
    sums_out[...] = jnp.concatenate(
        [jnp.sum(slope * normed, 0, keepdims=True), jnp.sum(slope, 0, keepdims=True)], 0
    )


def grad_kernel(linear, stats, sums, gain, slope, mask, grad_out):
    normed, inverse, count = normalise(linear[...], stats)
    grad_out[0] = (
        mask[...]
        * (gain[...] * inverse)
        * (slope[...] - (sums[1:2, :] + normed * sums[0:1, :]) / count)
    ).astype(jnp.bfloat16)


def back_kernel(grad, weight, counts_t, scale, own_out, halo_out):
    pieces, rows, piece = grad.shape
    total = dot(grad[0], weight[:, :piece], contract_columns)
    for b in range(1, pieces):
        total += dot(grad[b], weight[:, b * piece : (b + 1) * piece], contract_columns)
    weighted = (total * scale[...]).astype(jnp.bfloat16)
    own_out[...] = dot(counts_t[:rows], weighted)
    halo_out[...] = dot(counts_t[rows:], weighted).astype(jnp.bfloat16)


def last_kernel(own, pick_t, returned, out):
    out[...] = own[...] + dot(pick_t[...], returned[...])


def product_kernel(
    place, own, other, far, far_other, grad, grad_other, grad_far, send_out, keep_out
):
    rows = own.shape[1]
    total = dot(own[0], grad[0], contract_rows) + dot(other[0], grad_other[0], contract_rows)
    total += dot(far[0], grad_far[:rows], contract_rows)
    total += dot(far_other[0], grad_far[rows:], contract_rows)

    @pl.when(pl.program_id(0) == 0)
    def _():
        send_out[...] = total.astype(jnp.bfloat16)

    @pl.when(pl.program_id(0) == 1)
    def _():
        keep_out[...] = total


class WeightGradient:
    def __init__(self, mixed):
        self.dom, sub = lax.axis_index("dom"), lax.axis_index("sub")
        self.core, self.line, self.pair = sub & 1, sub >> 1, self.dom & 1
        self.links = (("sub", 2), ("dom", 1))
        self.mixed = mixed
        _, self.rows, self.piece = mixed.shape
        by_line = mixed.reshape(2, 2, self.rows, self.piece)
        shape = (2, self.rows, self.piece)
        self.to_share = [
            half(by_line, 0, 1 - self.line).reshape(shape),
            half(by_line, 1, 1 - self.pair).reshape(shape),
        ]

    def share(self, flow, start):
        self.to_share[flow] = swap(after(self.to_share[flow], start), *self.links[flow])

    def gather(self):
        self.far = self.to_share
        self.other = swap(self.mixed, "sub", 1)
        far_other = swap(jnp.concatenate(self.far), "sub", 1)
        self.far_other = (far_other[:2], far_other[2:])

    def split(self, grad):
        self.grad = half(grad, 0, self.core)
        self.grad_other = swap(half(grad, 0, 1 - self.core), "sub", 1)
        return self.grad_other

    def spread(self):
        pairs = jnp.concatenate([self.grad, self.grad_other], 1)
        self.grad_far = [
            swap(pairs[k], *self.links[k // splits]) for k in range(pairs.shape[0])
        ]

    def product(self, k):
        flow = k // splits
        piece, rows = self.piece, self.rows
        width = self.grad.shape[2]
        if flow == 0:
            keep, base, step = self.pair, 2 * self.line, 1
        else:
            keep, base, step = self.line, self.pair, 2
        place = jnp.stack([base + step * (1 - keep), base + step * keep, 1 - keep, keep])
        near = pl.BlockSpec((1, rows, piece), lambda i, at: (at[i], 0, 0))
        far = pl.BlockSpec((1, rows, piece), lambda i, at: (at[2 + i], 0, 0))
        grads = pl.BlockSpec((1, rows, width), lambda i, at: (k, 0, 0))
        return call(
            product_kernel,
            (2,),
            [near, near, far, far, grads, grads, whole((2 * rows, width))],
            [whole((piece, width))] * 2,
            [struct((piece, width), jnp.bfloat16), struct((piece, width))],
            16 * rows * piece * width,
            prefetch=1,
        )(
            place.astype(jnp.int32),
            self.mixed,
            self.other,
            self.far[flow],
            self.far_other[flow],
            self.grad,
            self.grad_other,
            self.grad_far[k],
        )

    def finish(self):
        chunks = 2 * splits
        bits = [1 << k for k in range(lax.axis_size("dom").bit_length() - 1)]
        rest = bits[1:]

        def at(bit):
            return (self.dom & bit) // bit

        products = [self.product(k) for k in range(chunks)]
        parts = [
            keep + swap(send, *self.links[1 - k // splits]).astype(jnp.float32)
            for k, (send, keep) in enumerate(products)
        ]
        for bit in rest[:-1]:
            for k in range(chunks):
                got = swap(rounded(half(parts[k], 0, 1 - at(bit))), "dom", bit)
                parts[k] = half(parts[k], 0, at(bit)) + got.astype(jnp.float32)
        for k in range(chunks):
            sent = rounded(parts[k])
            got = swap(sent, "dom", rest[-1]).astype(jnp.float32)
            parts[k] = rounded(sent.astype(jnp.float32) + got)[None]
        orders = []
        for k in range(chunks):
            order = [bit for bit in reversed(rest[:-1])] + [1]
            if k // splits and len(order) > 1:
                order[-2:] = [1, order[-2]]
            orders.append(order)
        for step in range(len(orders[0])):
            for k in range(chunks):
                bit = orders[k][step]
                got = swap(parts[k], "dom", bit)
                parts[k] = join(parts[k], got, 0 if bit == 1 else 1, at(bit))
        parts = jnp.concatenate(parts, 2)
        other = swap(half(parts, 0, 1 - self.core), "sub", 1)
        return join(half(parts, 0, self.core)[0], other[0], 1, self.core).astype(jnp.float32)


def on_device(
    features, weight, bn_gain, bn_shift, cotangent, neighbours, degrees, send_rows, valid_nodes
):
    rows, width = features.shape
    routes = send_rows.reshape(-1)
    halo = routes.shape[0]
    devices = lax.axis_size("dom") * lax.axis_size("sub")
    piece = width // 4
    steps = (width // tile,)

    def to_all(value):
        value = value.reshape(devices, halo // devices, width)
        return lax.all_to_all(value, both_axes, 0, 0, tiled=True).reshape(halo, width)

    pick = (
        routes[:, None] == lax.broadcasted_iota(jnp.int32, (halo, rows), 1)
    ).astype(jnp.bfloat16)
    outgoing = dot(pick, features).astype(jnp.bfloat16)
    arrived = to_all(outgoing)
    pick_t = (
        routes[None, :] == lax.broadcasted_iota(jnp.int32, (rows, halo), 0)
    ).astype(jnp.bfloat16)
    mask = valid_nodes.astype(jnp.float32)[:, None]
    scale = (1.0 / (degrees.astype(jnp.float32) + 1.0))[:, None]
    gain, shift = bn_gain[None, :], bn_shift[None, :]
    taken = lax.broadcasted_iota(jnp.int32, neighbours.shape, 1) < degrees[:, None]
    entries = jnp.where(taken, neighbours, -1)
    table = lax.broadcasted_iota(jnp.int32, (1, 1, rows + halo), 2)
    counts = jnp.sum((entries[:, :, None] == table).astype(jnp.float32), 1)
    counts = (counts + 2.0 * jnp.eye(rows, rows + halo, dtype=jnp.float32)).astype(jnp.bfloat16)
    counts_t = counts.T

    mixed, linear, stats = call(
        linear_kernel,
        steps,
        [
            whole(counts.shape),
            whole((rows, width)),
            whole((halo, width)),
            whole((rows, 1)),
            whole((rows, 1)),
            columns(width),
        ],
        [whole((4, rows, piece)), columns(rows), columns(3)],
        [struct((4, rows, piece), jnp.bfloat16), struct((rows, width)), struct((3, width))],
        2 * rows * width * (width + rows + halo),
        scratch=[pltpu.VMEM((rows, width), jnp.bfloat16)],
    )(counts, features, arrived, scale, mask, weight)

    product = WeightGradient(mixed)
    stats, merged = merge_statistics(stats)
    for flow in (0, 1):
        product.share(flow, merged[flow])

    active, slope, sums = call(
        gelu_kernel,
        steps,
        [columns(rows), columns(3), columns(1), columns(1), columns(rows), whole((rows, 1))],
        [columns(rows), columns(rows), columns(2)],
        [struct((rows, width), jnp.bfloat16), struct((rows, width)), struct((2, width))],
        40 * rows * width,
    )(linear, stats, gain, shift, cotangent, mask)
    sums, *product.to_share = lax.optimization_barrier((sums, *product.to_share))
    sums = sum_over_all(sums)

    grad_width = width // (4 * splits)
    grad = call(
        grad_kernel,
        (4 * splits,),
        [columns(rows, grad_width), columns(3, grad_width), columns(2, grad_width), columns(1, grad_width), columns(rows, grad_width), whole((rows, 1))],
        blocks(rows, grad_width),
        struct((4 * splits, rows, grad_width), jnp.bfloat16),
        10 * rows * width,
    )(linear, stats, sums, gain, slope, mask)
    product.gather()
    came = product.split(grad)
    product.spread()

    own_grad, halo_grad = call(
        back_kernel,
        steps,
        [
            whole(grad.shape),
            pl.BlockSpec((tile, width), lambda i: (i, 0)),
            whole(counts_t.shape),
            whole((rows, 1)),
        ],
        [columns(rows), columns(halo)],
        [struct((rows, width)), struct((halo, width), jnp.bfloat16)],
        2 * rows * width * (width + rows + halo),
    )(after(grad, came), weight, counts_t, scale)
    returned = to_all(halo_grad)
    grad_weight = product.finish()
    grad_features = call(
        last_kernel,
        steps,
        [columns(rows), whole((rows, halo)), columns(halo)],
        columns(rows),
        struct((rows, width)),
        2 * rows * width * halo,
    )(own_grad, pick_t, returned)
    return (active, grad_features, grad_weight, sums[0], sums[1])


def solution(mesh):
    return jax.shard_map(
        on_device,
        mesh=mesh,
        in_specs=(
            P(("dom", "sub"), None),
            P(),
            P(),
            P(),
            P(("dom", "sub"), None),
            P(("dom", "sub"), None),
            P(("dom", "sub")),
            P(("dom", "sub"), None, None, None),
            P(("dom", "sub")),
        ),
        out_specs=(P(("dom", "sub"), None), P(("dom", "sub"), None), P("sub", None), P(), P()),
        check_vma=False,
    )
```

```python
import functools
import math

import jax
import jax.numpy as jnp
from jax import lax
from jax.experimental import pallas as pl
from jax.experimental.pallas import tpu as pltpu
from jax.sharding import PartitionSpec as P

epsilon = 1e-05
both_axes = ("dom", "sub")
contract_rows = (((0,), (0,)), ((), ()))
contract_columns = (((1,), (1,)), ((), ()))


def swap(value, axis, offset):
    size = lax.axis_size(axis)
    return lax.ppermute(value, axis, [(i, i ^ offset) for i in range(size)])


def tree_sum(terms):
    while len(terms) > 1:
        terms = [terms[i] + terms[i + 1] for i in range(0, len(terms), 2)]
    return terms[0]


def exchange_steps():
    steps = []
    for axis in ("sub", "dom"):
        size, low = lax.axis_size(axis), 1
        odd = (size.bit_length() - 1) % 2
        while low < size:
            width = 2 if odd else 4
            odd = 0
            steps.append((axis, [low * k for k in range(1, width)]))
            low *= width
    return steps


def sum_over_all(value):
    for axis, offsets in exchange_steps():
        value = tree_sum([value] + [swap(value, axis, offset) for offset in offsets])
    return value


def merge_kernel(*refs):
    *parts, out = refs
    parts = [(p[0:1], p[1:2], p[2:3]) for p in parts]
    count = tree_sum([p[0] for p in parts])
    total = tree_sum([p[1] for p in parts])
    mean = total / jnp.maximum(count, 1.0)
    out[0:1] = count
    out[1:2] = total
    out[2:3] = tree_sum([p[2] + p[0] * jnp.square(p[1] / jnp.maximum(p[0], 1.0) - mean) for p in parts])


def merge_statistics(packed):
    steps = []
    for axis, offsets in exchange_steps():
        parts = [packed] + [swap(packed, axis, offset) for offset in offsets]
        packed = call(merge_kernel, struct(packed.shape), 30 * packed.size, *parts)
        steps.append(packed)
    return packed, steps


def after(value, *others):
    return lax.optimization_barrier((value,) + others)[0]


def place(bit):
    return (lax.axis_index("dom") // bit) % 2


def core_and_line():
    sub = lax.axis_index("sub")
    return sub % 2, sub // 2


def bytes_of(shapes):
    return sum(math.prod(s.shape) * s.dtype.itemsize for s in shapes)


def call(kernel, out_shape, flops, *operands):
    outs = out_shape if isinstance(out_shape, list) else [out_shape]
    vmem = pl.BlockSpec(memory_space=pltpu.VMEM)
    moved = bytes_of(operands) + bytes_of(outs)
    return pl.pallas_call(
        kernel,
        in_specs=[vmem] * len(operands),
        out_specs=[vmem] * len(outs) if isinstance(out_shape, list) else vmem,
        out_shape=out_shape,
        compiler_params=pltpu.CompilerParams(vmem_limit_bytes=6 * 2**20),
        cost_estimate=pl.CostEstimate(flops=flops, bytes_accessed=moved, transcendentals=0),
    )(*operands)


def struct(shape, dtype=jnp.float32):
    return jax.ShapeDtypeStruct(shape, dtype)


def dot(a, b, dims=(((1,), (0,)), ((), ()))):
    return lax.dot_general(a, b, dims, preferred_element_type=jnp.float32)


def tiles(length, width, body):
    def step(i, carry):
        body(i, pl.ds(pl.multiple_of(i * width, width), width))
        return carry

    lax.fori_loop(0, length // width, step, 0)


def pick_kernel(routes, features, out, pick_out):
    pick = (
        routes[...] == lax.broadcasted_iota(jnp.int32, pick_out.shape, 0)
    ).astype(jnp.bfloat16)
    pick_out[...] = pick

    def body(i, at):
        out[:, at] = dot(pick, features[:, at], contract_rows).astype(jnp.bfloat16)

    tiles(features.shape[1], 512, body)


def counts_kernel(neighbours, degrees, valid, counts_out, scale_out, mask_out):
    slots, rows = neighbours.shape
    table = counts_out.shape[0]
    step = 64

    def lanes_to_rows(value):
        return jnp.transpose(jnp.broadcast_to(value, (128, rows)))[:, :1]

    scale_out[...] = lanes_to_rows(1.0 / (degrees[...].astype(jnp.float32) + 1.0))
    mask_out[...] = lanes_to_rows(valid[...].astype(jnp.float32))
    own = lax.broadcasted_iota(jnp.int32, (1, rows), 1)

    def body(i, carry):
        at = pl.ds(pl.multiple_of(i * step, step), step)
        entry = i * step + lax.broadcasted_iota(jnp.int32, (step, rows), 0)
        total = jnp.where(entry == own, 2.0, 0.0)
        for k in range(slots):
            used = jnp.where(degrees[...] > k, neighbours[k : k + 1], -1)
            total += jnp.where(entry == used, 1.0, 0.0)
        counts_out[at] = total.astype(jnp.bfloat16)
        return carry

    lax.fori_loop(0, table // step, body, 0)


def linear_kernel(
    counts_t,
    features,
    arrived,
    scale,
    mask,
    weight,
    mixed_out,
    line_out,
    pair_out,
    linear_out,
    stats_out,
):
    rows, width = features.shape
    pieces, _, piece = mixed_out.shape
    for j in range(pieces):
        part = slice(j * piece, (j + 1) * piece)
        summed = dot(counts_t[:rows], features[:, part], contract_rows)
        summed += dot(counts_t[rows:], arrived[:, part], contract_rows)
        mixed_out[j] = (summed * scale[...]).astype(jnp.bfloat16)
    _, line = core_and_line()
    pair = place(1)
    for j in range(2):
        line_out[j] = mixed_out[2 * (1 - line) + j]
        pair_out[j] = mixed_out[2 * j + (1 - pair)]
    count = jnp.sum(mask[...])

    def body(i, at):
        linear = dot(mixed_out[0], weight[:piece, at])
        for j in range(1, pieces):
            linear += dot(mixed_out[j], weight[j * piece : (j + 1) * piece, at])
        linear_out[:, at] = linear
        total = jnp.sum(mask[...] * linear, 0, keepdims=True)
        off = linear - total / jnp.maximum(count, 1.0)
        stats_out[0:1, at] = jnp.full_like(total, count)
        stats_out[1:2, at] = total
        stats_out[2:3, at] = jnp.sum(mask[...] * off * off, 0, keepdims=True)

    tiles(width, 1024, body)


def column_terms(stats):
    count = stats[0:1]
    return stats[1:2] / count, lax.rsqrt(stats[2:3] / count + epsilon), count


def gelu_kernel(linear, stats, gain, shift, cotangent, mask, active_out, slope_out, sums_out):
    rows, width = linear.shape
    root, cubic = 0.7978845608028654, 0.044715

    def body(i, at):
        mean, inverse, _ = column_terms(stats[:, at])
        first = second = 0.0
        for r in range(0, rows, 64):
            here = slice(r, r + 64)
            normed = (linear[here, at] - mean) * inverse
            value = gain[:, at] * normed + shift[:, at]
            square = value * value
            bent = jnp.tanh(root * value * (1.0 + cubic * square))
            upper = 0.5 * (1.0 + bent)
            active_out[here, at] = (mask[here] * (value * upper)).astype(jnp.bfloat16)
            inner = 0.5 * root * value * (1.0 - bent * bent) * (1.0 + 3.0 * cubic * square)
            slope = mask[here] * cotangent[here, at].astype(jnp.float32) * (upper + inner)
            slope_out[here, at] = slope
            first = first + jnp.sum(slope * normed, 0, keepdims=True)
            second = second + jnp.sum(slope, 0, keepdims=True)
        sums_out[0:1, at] = first
        sums_out[1:2, at] = second

    tiles(width, 256, body)


def grad_kernel(linear, stats, sums, gain, slope, mask, grad_out, keep_out, send_out):
    rows, width = linear.shape
    pieces, _, piece = grad_out.shape

    def body(i, at):
        mean, inverse, count = column_terms(stats[:, at])
        factor = gain[:, at] * inverse
        along, offset = sums[0:1, at] / count, sums[1:2, at] / count
        for r in range(0, rows, 32):
            here = slice(r, r + 32)
            normed = (linear[here, at] - mean) * inverse
            grad_out[i, here] = (
                mask[here] * factor * (slope[here, at] - (offset + normed * along))
            ).astype(jnp.bfloat16)

    tiles(width, piece, body)
    core, _ = core_and_line()
    for j in range(pieces // 2):
        keep_out[j] = grad_out[core * (pieces // 2) + j]
        send_out[j] = grad_out[(1 - core) * (pieces // 2) + j]


def back_kernel(grad, weight, counts_t, scale, own_out, halo_out):
    pieces, rows, piece = grad.shape

    def body(i, at):
        total = dot(grad[0], weight[at, :piece], contract_columns)
        for b in range(1, pieces):
            total += dot(grad[b], weight[at, b * piece : (b + 1) * piece], contract_columns)
        weighted = (total * scale[...]).astype(jnp.bfloat16)
        own_out[:, at] = dot(counts_t[:rows], weighted)
        halo_out[:, at] = dot(counts_t[rows:], weighted).astype(jnp.bfloat16)

    tiles(weight.shape[0], 512, body)


def last_kernel(own, pick_t, returned, out):
    out[...] = own[...] + dot(pick_t[...], returned[...])


def product_kernel(
    flow, own, other, far, far_other, grad, grad_other, grad_far, grad_far_other, send_out, keep_out
):
    _, line = core_and_line()
    mine = (place(1), line)[flow]
    for which, out in ((1 - mine, send_out), (mine, keep_out)):
        near = (2 * line + which, 2 * which + place(1))[flow]
        total = dot(own[near], grad[...], contract_rows)
        total += dot(other[near], grad_other[...], contract_rows)
        total += dot(far[which], grad_far[...], contract_rows)
        total += dot(far_other[which], grad_far_other[...], contract_rows)
        out[...] = total.astype(out.dtype)


def split_kernel(bit, keep, got, send_out, keep_out):
    rows = keep_out.shape[0]
    mine = place(bit)
    for which, out in ((1 - mine, send_out), (mine, keep_out)):
        at = pl.ds(pl.multiple_of(which * rows, rows), rows)
        out[...] = (keep[at] + got[at].astype(jnp.float32)).astype(out.dtype)


def add_kernel(keep, got, out):
    out[...] = (keep[...].astype(jnp.float32) + got[...].astype(jnp.float32)).astype(out.dtype)


def join_kernel(bit, own, got, out):
    rows = own.shape[0]
    mine = place(bit)
    out[pl.ds(pl.multiple_of(mine * rows, rows), rows)] = own[...]
    out[pl.ds(pl.multiple_of((1 - mine) * rows, rows), rows)] = got[...]


def stack_kernel(own, got, out):
    out[0] = own[...]
    out[1] = got[...]


def sort_kernel(bit, own_first, got_first, own_second, got_second, send_out, keep_out):
    core, _ = core_and_line()
    pair, mine = place(1), place(bit)
    rows, width = own_first.shape
    part = rows // 2
    for block, out in ((1 - core, send_out), (core, keep_out)):
        own_block = block == pair

        @pl.when(own_block)
        def _():
            out[:, :width] = own_first[...]

        @pl.when(jnp.logical_not(own_block))
        def _():
            out[:, :width] = got_first[...]

        which = jnp.where(own_block, 0, 1)
        out[pl.ds(pl.multiple_of(mine * part, part), part), width:] = own_second[which]
        out[pl.ds(pl.multiple_of((1 - mine) * part, part), part), width:] = got_second[which]


def place_kernel(own, got, out):
    core, _ = core_and_line()
    width = own.shape[1]
    out[:, pl.ds(pl.multiple_of(core * width, width), width)] = own[...].astype(jnp.float32)
    out[:, pl.ds(pl.multiple_of((1 - core) * width, width), width)] = got[...].astype(jnp.float32)


class WeightGradient:
    def __init__(self, mixed, to_share):
        self.mixed, self.to_share = mixed, list(to_share)
        _, self.rows, self.piece = mixed.shape

    def over(self, flow, value):
        return swap(value, "sub", 2) if flow == 0 else swap(value, "dom", 1)

    def over_and_core(self, flow, value):
        if flow == 0:
            return swap(value, "sub", 3)
        subs = lax.axis_size("sub")
        size = lax.axis_size("dom") * subs
        return lax.ppermute(value, both_axes, [(i, i ^ (subs + 1)) for i in range(size)])

    def share(self, flow, start):
        self.to_share[flow] = self.over(flow, after(self.to_share[flow], start))

    def gather(self):
        self.far = self.to_share
        self.other = swap(self.mixed, "sub", 1)
        self.far_other = [swap(far, "sub", 1) for far in self.far]

    def spread(self, keep, send):
        self.grad = keep
        self.grad_far = [self.over(flow, keep[flow]) for flow in (0, 1)]
        self.grad_far_other = [self.over_and_core(flow, send[flow]) for flow in (0, 1)]
        self.grad_other = swap(send, "sub", 1)

    def product(self, flow):
        piece, rows = self.piece, self.rows
        width = self.grad.shape[2]
        return call(
            functools.partial(product_kernel, flow),
            [struct((piece, width), jnp.bfloat16), struct((piece, width))],
            16 * rows * piece * width,
            self.mixed,
            self.other,
            self.far[flow],
            self.far_other[flow],
            self.grad[flow],
            self.grad_other[flow],
            self.grad_far[flow],
            self.grad_far_other[flow],
        )

    def finish(self):
        bits = [1 << k for k in range(lax.axis_size("dom").bit_length() - 1)]
        rest = bits[1:]
        flows = (0, 1)
        sends, parts = zip(*[self.product(flow) for flow in flows])
        gots = [self.over(1 - flow, sends[flow]) for flow in flows]
        parts = list(parts)
        for bit in rest[:-1]:
            for flow in flows:
                rows, width = parts[flow].shape
                send, parts[flow] = call(
                    functools.partial(split_kernel, bit),
                    [struct((rows // 2, width), jnp.bfloat16), struct((rows // 2, width))],
                    rows * width,
                    parts[flow],
                    gots[flow],
                )
                gots[flow] = swap(send, "dom", bit)
        for flow in flows:
            shape = parts[flow].shape
            sent = call(add_kernel, struct(shape, jnp.bfloat16), 1000, parts[flow], gots[flow])
            got = swap(sent, "dom", rest[-1])
            parts[flow] = call(add_kernel, struct(shape, jnp.bfloat16), 1000, sent, got)

        def join(part, bit):
            rows, width = part.shape
            return call(
                functools.partial(join_kernel, bit),
                struct((2 * rows, width), jnp.bfloat16),
                rows * width,
                part,
                swap(part, "dom", bit),
            )

        first, second = parts
        for bit in reversed(rest[1:-1]):
            first, second = join(first, bit), join(second, bit)
        second_got = swap(second, "dom", 1)
        first = join(first, rest[0])
        second = call(
            stack_kernel, struct((2,) + second.shape, jnp.bfloat16), second.size, second, second_got
        )
        first_got, second_got = swap(first, "dom", 1), swap(second, "dom", rest[0])
        rows, width = first.shape
        send, keep = call(
            functools.partial(sort_kernel, rest[0]),
            [struct((rows, 2 * width), jnp.bfloat16)] * 2,
            first.size,
            first,
            first_got,
            second,
            second_got,
        )
        return call(
            place_kernel, struct((rows, 4 * width)), 4 * first.size, keep, swap(send, "sub", 1)
        )


def on_device(
    features, weight, bn_gain, bn_shift, cotangent, neighbours, degrees, send_rows, valid_nodes
):
    rows, width = features.shape
    routes = send_rows.reshape(-1)
    halo = routes.shape[0]
    devices = lax.axis_size("dom") * lax.axis_size("sub")
    piece = width // 4

    def to_all(value):
        value = value.reshape(devices, halo // devices, width)
        return lax.all_to_all(value, both_axes, 0, 0, tiled=True).reshape(halo, width)

    outgoing, pick_t = call(
        pick_kernel,
        [struct((halo, width), jnp.bfloat16), struct((rows, halo), jnp.bfloat16)],
        2 * halo * rows * width,
        routes[None, :],
        features,
    )
    arrived = to_all(outgoing)
    gain, shift = bn_gain[None, :], bn_shift[None, :]
    counts_t, scale, mask = call(
        counts_kernel,
        [struct((rows + halo, rows), jnp.bfloat16), struct((rows, 1)), struct((rows, 1))],
        3 * neighbours.size * (rows + halo),
        neighbours.T,
        degrees[None, :],
        valid_nodes[None, :],
    )

    share = struct((2, rows, piece), jnp.bfloat16)
    mixed, *to_share, linear, stats = call(
        linear_kernel,
        [
            struct((4, rows, piece), jnp.bfloat16),
            share,
            share,
            struct((rows, width)),
            struct((3, width)),
        ],
        2 * rows * width * (width + rows + halo),
        counts_t,
        features,
        arrived,
        scale,
        mask,
        weight,
    )

    product = WeightGradient(mixed, to_share)
    stats, merged = merge_statistics(stats)
    for flow in (0, 1):
        product.share(flow, merged[flow])

    active, slope, sums = call(
        gelu_kernel,
        [struct((rows, width), jnp.bfloat16), struct((rows, width)), struct((2, width))],
        40 * rows * width,
        linear,
        stats,
        gain,
        shift,
        cotangent,
        mask,
    )
    sums, *product.to_share = lax.optimization_barrier((sums, *product.to_share))
    sums = sum_over_all(sums)

    blocks = struct((2, rows, piece), jnp.bfloat16)
    grad, keep, send = call(
        grad_kernel,
        [struct((4, rows, piece), jnp.bfloat16), blocks, blocks],
        10 * rows * width,
        linear,
        stats,
        sums,
        gain,
        slope,
        mask,
    )
    product.gather()
    product.spread(keep, send)
    own_grad, halo_grad = call(
        back_kernel,
        [struct((rows, width)), struct((halo, width), jnp.bfloat16)],
        2 * rows * width * (width + rows + halo),
        grad,
        weight,
        counts_t,
        scale,
    )
    returned = to_all(halo_grad)
    product.grad_far = [after(v, halo_grad) for v in product.grad_far]
    grad_weight = product.finish()
    grad_features = call(
        last_kernel, struct((rows, width)), 2 * rows * width * halo, own_grad, pick_t, returned
    )
    return (active, grad_features, grad_weight, sums[0], sums[1])


def solution(mesh):
    return jax.shard_map(
        on_device,
        mesh=mesh,
        in_specs=(
            P(("dom", "sub"), None),
            P(),
            P(),
            P(),
            P(("dom", "sub"), None),
            P(("dom", "sub"), None),
            P(("dom", "sub")),
            P(("dom", "sub"), None, None, None),
            P(("dom", "sub")),
        ),
        out_specs=(P(("dom", "sub"), None), P(("dom", "sub"), None), P("sub", None), P(), P()),
        check_vma=False,
    )
```

```python
import functools
import math

import jax
import jax.numpy as jnp
from jax import lax
from jax.experimental import pallas as pl
from jax.experimental.pallas import tpu as pltpu
from jax.sharding import PartitionSpec as P

epsilon = 1e-05
splits = 2
ahead = 1
tie = None
both_axes = ("dom", "sub")
contract_rows = (((0,), (0,)), ((), ()))
contract_columns = (((1,), (1,)), ((), ()))


def swap(value, axis, offset):
    size = lax.axis_size(axis)
    return lax.ppermute(value, axis, [(i, i ^ offset) for i in range(size)])


def tree_sum(terms):
    while len(terms) > 1:
        terms = [terms[i] + terms[i + 1] for i in range(0, len(terms), 2)]
    return terms[0]


def exchange_steps():
    steps = []
    for axis in ("sub", "dom"):
        size, low = lax.axis_size(axis), 1
        odd = (size.bit_length() - 1) % 2
        while low < size:
            width = 2 if odd else 4
            odd = 0
            steps.append((axis, [low * k for k in range(1, width)]))
            low *= width
    return steps


def sum_over_all(value):
    for axis, offsets in exchange_steps():
        value = tree_sum([value] + [swap(value, axis, offset) for offset in offsets])
    return value


def merge_kernel(*refs):
    *parts, out = refs
    parts = [(p[0:1], p[1:2], p[2:3]) for p in parts]
    count = tree_sum([p[0] for p in parts])
    total = tree_sum([p[1] for p in parts])
    mean = total / jnp.maximum(count, 1.0)
    out[0:1] = count
    out[1:2] = total
    out[2:3] = tree_sum([p[2] + p[0] * jnp.square(p[1] / jnp.maximum(p[0], 1.0) - mean) for p in parts])


def merge_statistics(packed):
    steps = []
    for axis, offsets in exchange_steps():
        parts = [packed] + [swap(packed, axis, offset) for offset in offsets]
        packed = call(merge_kernel, struct(packed.shape), 30 * packed.size, *parts)
        steps.append(packed)
    return packed, steps


def after(value, *others):
    return lax.optimization_barrier((value,) + others)[0]


def place(bit):
    return (lax.axis_index("dom") // bit) % 2


def core_and_line():
    sub = lax.axis_index("sub")
    return sub % 2, sub // 2


def bytes_of(shapes):
    return sum(math.prod(s.shape) * s.dtype.itemsize for s in shapes)


def call(
    kernel, out_shape, flops, *operands, far=(), far_out=(), near_out=(), scratch=(), vmem=6, alias=None
):
    several = isinstance(out_shape, list)
    outs = out_shape if several else [out_shape]

    def specs(count, away):
        return [
            pl.BlockSpec(memory_space=pltpu.HBM if i in away else pltpu.VMEM) for i in range(count)
        ]

    out_specs = specs(len(outs), far_out)
    results = list(outs)
    for i in far_out:
        results[i] = pltpu.HBM(outs[i].shape, outs[i].dtype)
    for i in near_out:
        results[i] = pltpu.VMEM(outs[i].shape, outs[i].dtype)
    operands = [
        pltpu.with_memory_space_constraint(x, pltpu.HBM) if i in far else x
        for i, x in enumerate(operands)
    ]
    return pl.pallas_call(
        kernel,
        in_specs=specs(len(operands), far),
        out_specs=out_specs if several else out_specs[0],
        out_shape=results if several else results[0],
        scratch_shapes=scratch,
        input_output_aliases=alias or {},
        compiler_params=pltpu.CompilerParams(vmem_limit_bytes=vmem * 2**20),
        cost_estimate=pl.CostEstimate(
            flops=flops, bytes_accessed=bytes_of(operands) + bytes_of(outs), transcendentals=0
        ),
    )(*operands)


def struct(shape, dtype=jnp.float32):
    return jax.ShapeDtypeStruct(shape, dtype)


def dot(a, b, dims=(((1,), (0,)), ((), ()))):
    return lax.dot_general(a, b, dims, preferred_element_type=jnp.float32)


def tiles(length, width, body):
    def step(i, carry):
        body(i, pl.ds(pl.multiple_of(i * width, width), width))
        return carry

    lax.fori_loop(0, length // width, step, 0)


def column_tiles(array, width):
    return [array.at[:, pl.ds(j * width, width)] for j in range(array.shape[1] // width)]


def picked(routes, rows):
    devices, slots = routes.shape
    halo = devices * slots
    slot_of = lax.broadcasted_iota(jnp.int32, (slots, halo), 1) % slots
    spread = (slot_of == lax.broadcasted_iota(jnp.int32, (slots, halo), 0)).astype(jnp.bfloat16)
    by_device = dot(routes[...].astype(jnp.float32).astype(jnp.bfloat16), spread)
    device_of = lax.broadcasted_iota(jnp.int32, (devices, halo), 1) // slots
    here = device_of == lax.broadcasted_iota(jnp.int32, (devices, halo), 0)
    wanted = jnp.sum(jnp.where(here, by_device, 0.0), 0, keepdims=True).astype(jnp.int32)
    return (wanted == lax.broadcasted_iota(jnp.int32, (rows, halo), 0)).astype(jnp.bfloat16)


def pick_kernel(routes, features, out, features_here, out_here, arrive, leave):
    inward = [
        pltpu.make_async_copy(*refs, arrive.at[j])
        for j, refs in enumerate(
            zip(column_tiles(features, 512), column_tiles(features_here, 512))
        )
    ]
    outward = [
        pltpu.make_async_copy(*refs, leave.at[j])
        for j, refs in enumerate(zip(column_tiles(out_here, 512), column_tiles(out, 512)))
    ]
    for copy in inward:
        copy.start()
    pick = picked(routes, features.shape[0])
    for j, copy in enumerate(inward):
        copy.wait()
        at = slice(j * 512, (j + 1) * 512)
        out_here[:, at] = dot(pick, features_here[:, at], contract_rows).astype(jnp.bfloat16)
        outward[j].start()
    for copy in outward:
        copy.wait()


def counts_kernel(
    neighbours, degrees, valid, routes, counts_out, scale_out, mask_out, pick_out
):
    slots, rows = neighbours.shape
    table = counts_out.shape[0]
    pick_out[...] = picked(routes, rows)
    step = 64

    def lanes_to_rows(value):
        return jnp.transpose(jnp.broadcast_to(value, (128, rows)))[:, :1]

    scale_out[...] = lanes_to_rows(1.0 / (degrees[...].astype(jnp.float32) + 1.0))
    mask_out[...] = lanes_to_rows(valid[...].astype(jnp.float32))
    own = lax.broadcasted_iota(jnp.int32, (1, rows), 1)

    def body(i, carry):
        at = pl.ds(pl.multiple_of(i * step, step), step)
        entry = i * step + lax.broadcasted_iota(jnp.int32, (step, rows), 0)
        total = jnp.where(entry == own, 2.0, 0.0)
        for k in range(slots):
            used = jnp.where(degrees[...] > k, neighbours[k : k + 1], -1)
            total += jnp.where(entry == used, 1.0, 0.0)
        counts_out[at] = total.astype(jnp.bfloat16)
        return carry

    lax.fori_loop(0, table // step, body, 0)


def linear_kernel(
    counts_t,
    features,
    arrived,
    scale,
    mask,
    weight,
    mixed_out,
    line_out,
    pair_out,
    linear_out,
    stats_out,
    weight_here,
    arrive,
):
    tile = 512
    copies = [
        pltpu.make_async_copy(*refs, arrive.at[j])
        for j, refs in enumerate(zip(column_tiles(weight, tile), column_tiles(weight_here, tile)))
    ]
    for copy in copies:
        copy.start()
    rows, width = features.shape
    pieces, _, piece = mixed_out.shape
    for j in range(pieces):
        part = slice(j * piece, (j + 1) * piece)
        summed = dot(counts_t[:rows], features[:, part], contract_rows)
        summed += dot(counts_t[rows:], arrived[:, part], contract_rows)
        mixed_out[j] = (summed * scale[...]).astype(jnp.bfloat16)
    _, line = core_and_line()
    pair = place(1)
    for j in range(2):
        line_out[j] = mixed_out[2 * (1 - line) + j]
        pair_out[j] = mixed_out[2 * j + (1 - pair)]
    count = jnp.sum(mask[...])
    for i, copy in enumerate(copies):
        copy.wait()
        at = slice(i * tile, (i + 1) * tile)
        linear = dot(mixed_out[0], weight_here[:piece, at])
        for j in range(1, pieces):
            linear += dot(mixed_out[j], weight_here[j * piece : (j + 1) * piece, at])
        linear_out[:, at] = linear
        total = jnp.sum(mask[...] * linear, 0, keepdims=True)
        off = linear - total / jnp.maximum(count, 1.0)
        stats_out[0:1, at] = jnp.full_like(total, count)
        stats_out[1:2, at] = total
        stats_out[2:3, at] = jnp.sum(mask[...] * off * off, 0, keepdims=True)


def column_terms(stats):
    count = stats[0:1]
    return stats[1:2] / count, lax.rsqrt(stats[2:3] / count + epsilon), count


def gelu_kernel(linear, stats, gain, shift, cotangent, mask, active_out, slope_out, sums_out):
    rows, width = linear.shape
    root, cubic = 0.7978845608028654, 0.044715

    def body(i, at):
        mean, inverse, _ = column_terms(stats[:, at])
        first = second = 0.0
        for r in range(0, rows, 64):
            here = slice(r, r + 64)
            normed = (linear[here, at] - mean) * inverse
            value = gain[:, at] * normed + shift[:, at]
            square = value * value
            bent = jnp.tanh(root * value * (1.0 + cubic * square))
            upper = 0.5 * (1.0 + bent)
            active_out[here, at] = (mask[here] * (value * upper)).astype(jnp.bfloat16)
            inner = 0.5 * root * value * (1.0 - bent * bent) * (1.0 + 3.0 * cubic * square)
            slope = mask[here] * cotangent[here, at].astype(jnp.float32) * (upper + inner)
            slope_out[here, at] = slope
            first = first + jnp.sum(slope * normed, 0, keepdims=True)
            second = second + jnp.sum(slope, 0, keepdims=True)
        sums_out[0:1, at] = first
        sums_out[1:2, at] = second

    tiles(width, 256, body)


def grad_kernel(linear, stats, sums, gain, slope, mask, grad_out, keep_out, send_out):
    rows, width = linear.shape
    pieces, _, piece = grad_out.shape

    def body(i, at):
        mean, inverse, count = column_terms(stats[:, at])
        factor = gain[:, at] * inverse
        along, offset = sums[0:1, at] / count, sums[1:2, at] / count
        for r in range(0, rows, 32):
            here = slice(r, r + 32)
            normed = (linear[here, at] - mean) * inverse
            grad_out[i, here] = (
                mask[here] * factor * (slope[here, at] - (offset + normed * along))
            ).astype(jnp.bfloat16)

    tiles(width, piece, body)
    core, _ = core_and_line()
    width = keep_out.shape[2]
    chunks = piece // width
    for j in range(pieces // 2):
        for c in range(chunks):
            part = slice(c * width, (c + 1) * width)
            keep_out[j * chunks + c] = grad_out[core * (pieces // 2) + j, :, part]
            send_out[j * chunks + c] = grad_out[(1 - core) * (pieces // 2) + j, :, part]


def back_kernel(grad, weight, counts_t, scale, own, halo, own_here, halo_here, leave):
    pieces, rows, piece = grad.shape
    tile = 512
    outward = []
    for i in range(weight.shape[0] // tile):
        at = slice(i * tile, (i + 1) * tile)
        total = dot(grad[0], weight[at, :piece], contract_columns)
        for b in range(1, pieces):
            total += dot(grad[b], weight[at, b * piece : (b + 1) * piece], contract_columns)
        weighted = (total * scale[...]).astype(jnp.bfloat16)
        halo_here[:, at] = dot(counts_t[rows:], weighted).astype(jnp.bfloat16)
        own_here[:, at] = dot(counts_t[:rows], weighted)
        for k, refs in enumerate(((halo_here, halo), (own_here, own))):
            source, target = (ref.at[:, pl.ds(i * tile, tile)] for ref in refs)
            outward.append(pltpu.make_async_copy(source, target, leave.at[2 * i + k]))
            outward[-1].start()
    for copy in outward:
        copy.wait()


def last_kernel(own, pick_t, returned, out):
    out[...] = own[...] + dot(pick_t[...], returned[...])


def product_kernel(flow, own, other, far, far_other, grad, grad_far, send_out, keep_out):
    _, line = core_and_line()
    mine = (place(1), line)[flow]
    rows = own.shape[1]
    for which, out in ((1 - mine, send_out), (mine, keep_out)):
        near = (2 * line + which, 2 * which + place(1))[flow]
        total = dot(own[near], grad[:rows], contract_rows)
        total += dot(other[near], grad[rows:], contract_rows)
        total += dot(far[which], grad_far[:rows], contract_rows)
        total += dot(far_other[which], grad_far[rows:], contract_rows)
        out[...] = total.astype(out.dtype)


def split_kernel(bit, keep, got, send_out, keep_out):
    rows = keep_out.shape[0]
    mine = place(bit)
    for which, out in ((1 - mine, send_out), (mine, keep_out)):
        at = pl.ds(pl.multiple_of(which * rows, rows), rows)
        out[...] = (keep[at] + got[at].astype(jnp.float32)).astype(out.dtype)


def add_kernel(keep, got, out):
    out[...] = (keep[...].astype(jnp.float32) + got[...].astype(jnp.float32)).astype(out.dtype)


def join_kernel(bit, own, got, out):
    rows = own.shape[0]
    mine = place(bit)
    out[pl.ds(pl.multiple_of(mine * rows, rows), rows)] = own[...]
    out[pl.ds(pl.multiple_of((1 - mine) * rows, rows), rows)] = got[...]


def stack_kernel(own, got, out):
    out[0] = own[...]
    out[1] = got[...]


def sort_kernel(bit, *refs):
    *gathered, send_out, keep_out = refs
    chunks = len(gathered) // 4
    core, _ = core_and_line()
    pair, mine = place(1), place(bit)
    rows, width = gathered[0].shape
    part = rows // 2
    for block, out in ((1 - core, send_out), (core, keep_out)):
        own_block = block == pair
        which = jnp.where(own_block, 0, 1)
        for chunk in range(chunks):
            own_first, got_first, own_second, got_second = gathered[4 * chunk : 4 * chunk + 4]
            first = pl.ds(chunk * width, width)
            second = pl.ds((chunks + chunk) * width, width)

            @pl.when(own_block)
            def _():
                out[:, first] = own_first[...]

            @pl.when(jnp.logical_not(own_block))
            def _():
                out[:, first] = got_first[...]

            out[pl.ds(pl.multiple_of(mine * part, part), part), second] = own_second[which]
            out[pl.ds(pl.multiple_of((1 - mine) * part, part), part), second] = got_second[which]


def place_own_kernel(part, out, wide, leave):
    core, _ = core_and_line()
    place_half(core, part, out, wide, leave)


def place_other_kernel(part, _, out, wide, leave):
    core, _ = core_and_line()
    place_half(1 - core, part, out, wide, leave)


def place_half(which, part, out, wide, leave):
    rows, width = part.shape
    height = rows // 4
    copies = []
    for j in range(4):
        here = pl.ds(j * height, height)
        wide[here] = part[here].astype(jnp.float32)
        target = out.at[here, pl.ds(pl.multiple_of(which * width, width), width)]
        copies.append(pltpu.make_async_copy(wide.at[here], target, leave.at[j]))
        copies[-1].start()
    for copy in copies:
        copy.wait()


def pair_kernel(keep, other, *outs):
    rows = keep.shape[1]
    for k, out in enumerate(outs):
        out[:rows] = keep[k]
        out[rows:] = other[k]


class WeightGradient:
    def __init__(self, mixed, to_share):
        self.mixed, self.to_share = mixed, list(to_share)
        _, self.rows, self.piece = mixed.shape
        self.ended = {}

    def over(self, flow, value):
        return swap(value, "sub", 2) if flow == 0 else swap(value, "dom", 1)

    def share(self, flow, start):
        self.to_share[flow] = self.over(flow, after(self.to_share[flow], start))

    def gather(self):
        self.far = self.to_share
        self.other = swap(self.mixed, "sub", 1)
        self.far_other = [swap(far, "sub", 1) for far in self.far]

    def ordered(self, key, chunk, value, move):
        if chunk >= ahead:
            value = after(value, self.ended[key, chunk - ahead])
        value = move(value)
        self.ended[key, chunk] = value
        return value

    def spread(self, keep, send):
        count, rows, width = keep.shape
        other = swap(send, "sub", 1)
        self.near = call(
            pair_kernel, [struct((2 * rows, width), jnp.bfloat16)] * count, 1000, keep, other
        )
        self.grad_far = {}
        for chunk in range(splits):
            for flow in (0, 1):
                self.grad_far[flow, chunk] = self.ordered(
                    ("spread", flow),
                    chunk,
                    self.near[flow * splits + chunk],
                    functools.partial(self.over, flow),
                )

    def product(self, flow, chunk, gate):
        piece, rows = self.piece, self.rows
        far = self.grad_far[flow, chunk]
        width = far.shape[1]
        return call(
            functools.partial(product_kernel, flow),
            [struct((piece, width), jnp.bfloat16), struct((piece, width))],
            16 * rows * piece * width,
            self.mixed,
            self.other,
            self.far[flow],
            self.far_other[flow],
            self.near[flow * splits + chunk],
            after(far, gate),
        )

    def finish(self, gate, returned):
        bits = [1 << k for k in range(lax.axis_size("dom").bit_length() - 1)]
        rest = bits[1:]
        flows = (0, 1)
        gathered = []
        for chunk in range(splits):

            def move(name, flow, value, axis, bit):
                nonlocal returned
                if tie == (name, flow, chunk):
                    value, returned = lax.optimization_barrier((value, returned))
                return self.ordered((name, flow), chunk, value, lambda v: swap(v, axis, bit))

            sends, parts = zip(*[self.product(flow, chunk, gate) for flow in flows])
            links = (("dom", 1), ("sub", 2))
            gots = [move("sum", flow, sends[flow], *links[flow]) for flow in flows]
            parts = list(parts)
            for bit in rest[:-1]:
                for flow in flows:
                    rows, width = parts[flow].shape
                    send, parts[flow] = call(
                        functools.partial(split_kernel, bit),
                        [struct((rows // 2, width), jnp.bfloat16), struct((rows // 2, width))],
                        rows * width,
                        parts[flow],
                        gots[flow],
                    )
                    gots[flow] = move(f"sum{bit}", flow, send, "dom", bit)
            for flow in flows:
                shape = parts[flow].shape
                sent = call(add_kernel, struct(shape, jnp.bfloat16), 1000, parts[flow], gots[flow])
                got = move("last", flow, sent, "dom", rest[-1])
                parts[flow] = call(add_kernel, struct(shape, jnp.bfloat16), 1000, sent, got)

            def join(part, flow, bit):
                rows, width = part.shape
                return call(
                    functools.partial(join_kernel, bit),
                    struct((2 * rows, width), jnp.bfloat16),
                    rows * width,
                    part,
                    move(f"join{bit}", flow, part, "dom", bit),
                )

            first, second = parts
            for bit in reversed(rest[1:-1]):
                first, second = join(first, 0, bit), join(second, 1, bit)
            second_got = move("pair", 1, second, "dom", 1)
            first = join(first, 0, rest[0])
            second = call(
                stack_kernel,
                struct((2,) + second.shape, jnp.bfloat16),
                second.size,
                second,
                second_got,
            )
            first_got = move("pair", 0, first, "dom", 1)
            second_got = move(f"join{rest[0]}", 1, second, "dom", rest[0])
            gathered += [first, first_got, second, second_got]
        rows, width = first.shape
        send, keep = call(
            functools.partial(sort_kernel, rest[0]),
            [struct((rows, 2 * splits * width), jnp.bfloat16)] * 2,
            splits * first.size,
            *gathered,
        )
        shape = struct((rows, 4 * splits * width))
        scratch = [pltpu.VMEM(keep.shape, jnp.float32), pltpu.SemaphoreType.DMA((4,))]
        other = swap(send, "sub", 1)
        out = call(place_own_kernel, shape, first.size, keep, far_out=(0,), scratch=scratch)
        out = call(
            place_other_kernel,
            shape,
            first.size,
            other,
            out,
            far=(1,),
            far_out=(0,),
            scratch=scratch,
            alias={1: 0},
        )
        return out, returned


def on_device(
    features, weight, bn_gain, bn_shift, cotangent, neighbours, degrees, send_rows, valid_nodes
):
    rows, width = features.shape
    halo = send_rows.size
    devices = lax.axis_size("dom") * lax.axis_size("sub")
    piece = width // 4

    def to_all(value):
        value = value.reshape(devices, halo // devices, width)
        return lax.all_to_all(value, both_axes, 0, 0, tiled=True).reshape(halo, width)

    routes = send_rows.reshape(devices, halo // devices)
    outgoing = call(
        pick_kernel,
        struct((halo, width), jnp.bfloat16),
        2 * halo * rows * width,
        routes,
        features,
        far=(1,),
        far_out=(0,),
        scratch=[
            pltpu.VMEM((rows, width), jnp.bfloat16),
            pltpu.VMEM((halo, width), jnp.bfloat16),
            pltpu.SemaphoreType.DMA((width // 512,)),
            pltpu.SemaphoreType.DMA((width // 512,)),
        ],
        vmem=6 + (halo * width >> 19),
    )
    arrived = to_all(outgoing)
    gain, shift = bn_gain[None, :], bn_shift[None, :]
    counts_t, scale, mask, pick_t = call(
        counts_kernel,
        [
            struct((rows + halo, rows), jnp.bfloat16),
            struct((rows, 1)),
            struct((rows, 1)),
            struct((rows, halo), jnp.bfloat16),
        ],
        3 * neighbours.size * (rows + halo),
        neighbours.T,
        degrees[None, :],
        valid_nodes[None, :],
        routes,
    )

    share = struct((2, rows, piece), jnp.bfloat16)
    mixed, *to_share, linear, stats, weight_here = call(
        linear_kernel,
        [
            struct((4, rows, piece), jnp.bfloat16),
            share,
            share,
            struct((rows, width)),
            struct((3, width)),
            struct(weight.shape, jnp.bfloat16),
        ],
        2 * rows * width * (width + rows + halo),
        counts_t,
        features,
        arrived,
        scale,
        mask,
        weight,
        far=(5,),
        near_out=(5,),
        scratch=[pltpu.SemaphoreType.DMA((width // 512,))],
    )

    product = WeightGradient(mixed, to_share)
    stats, merged = merge_statistics(stats)
    for flow in (0, 1):
        product.share(flow, merged[flow])

    active, slope, sums = call(
        gelu_kernel,
        [struct((rows, width), jnp.bfloat16), struct((rows, width)), struct((2, width))],
        40 * rows * width,
        linear,
        stats,
        gain,
        shift,
        cotangent,
        mask,
    )
    sums, *product.to_share = lax.optimization_barrier((sums, *product.to_share))
    sums = sum_over_all(sums)

    blocks = struct((2 * splits, rows, piece // splits), jnp.bfloat16)
    grad, keep, send = call(
        grad_kernel,
        [struct((4, rows, piece), jnp.bfloat16), blocks, blocks],
        10 * rows * width,
        linear,
        stats,
        sums,
        gain,
        slope,
        mask,
    )
    product.gather()
    product.spread(keep, send)
    own_grad, halo_grad = call(
        back_kernel,
        [struct((rows, width)), struct((halo, width), jnp.bfloat16)],
        2 * rows * width * (width + rows + halo),
        grad,
        weight_here,
        counts_t,
        scale,
        far_out=(0, 1),
        scratch=[
            pltpu.VMEM((rows, width), jnp.float32),
            pltpu.VMEM((halo, width), jnp.bfloat16),
            pltpu.SemaphoreType.DMA((2 * width // 512,)),
        ],
        vmem=6 + (halo * width >> 19),
    )
    returned = to_all(halo_grad)
    grad_weight, returned = product.finish(halo_grad, returned)
    grad_features = call(
        last_kernel, struct((rows, width)), 2 * rows * width * halo, own_grad, pick_t, returned
    )
    return (active, grad_features, grad_weight, sums[0], sums[1])


def solution(mesh):
    return jax.shard_map(
        on_device,
        mesh=mesh,
        in_specs=(
            P(("dom", "sub"), None),
            P(),
            P(),
            P(),
            P(("dom", "sub"), None),
            P(("dom", "sub"), None),
            P(("dom", "sub")),
            P(("dom", "sub"), None, None, None),
            P(("dom", "sub")),
        ),
        out_specs=(P(("dom", "sub"), None), P(("dom", "sub"), None), P("sub", None), P(), P()),
        check_vma=False,
    )
```

```python
import functools
import math

import jax
import jax.numpy as jnp
from jax import lax
from jax.experimental import pallas as pl
from jax.experimental.pallas import tpu as pltpu
from jax.sharding import PartitionSpec as P

epsilon = 1e-05
chunk_widths = (256, 256)
splits = len(chunk_widths)
lag = 1
both_axes = ("dom", "sub")
contract_rows = (((0,), (0,)), ((), ()))
contract_columns = (((1,), (1,)), ((), ()))


def swap(value, axis, offset):
    size = lax.axis_size(axis)
    return lax.ppermute(value, axis, [(i, i ^ offset) for i in range(size)])


def tree_sum(terms):
    while len(terms) > 1:
        terms = [terms[i] + terms[i + 1] for i in range(0, len(terms), 2)]
    return terms[0]


def exchange_steps():
    steps = []
    for axis in ("sub", "dom"):
        size, low = lax.axis_size(axis), 1
        odd = (size.bit_length() - 1) % 2
        while low < size:
            width = 2 if odd else 4
            odd = 0
            steps.append((axis, [low * k for k in range(1, width)]))
            low *= width
    return steps


def sum_over_all(value):
    for axis, offsets in exchange_steps():
        value = tree_sum([value] + [swap(value, axis, offset) for offset in offsets])
    return value


def merge_kernel(*refs):
    *parts, out = refs
    parts = [(p[0:1], p[1:2], p[2:3]) for p in parts]
    count = tree_sum([p[0] for p in parts])
    total = tree_sum([p[1] for p in parts])
    mean = total / jnp.maximum(count, 1.0)
    out[0:1] = count
    out[1:2] = total
    out[2:3] = tree_sum([p[2] + p[0] * jnp.square(p[1] / jnp.maximum(p[0], 1.0) - mean) for p in parts])


def merge_statistics(packed):
    steps = []
    for axis, offsets in exchange_steps():
        parts = [packed] + [swap(packed, axis, offset) for offset in offsets]
        packed = call(merge_kernel, struct(packed.shape), 30 * packed.size, *parts)
        steps.append(packed)
    return packed, steps


def after(value, *others):
    return lax.optimization_barrier((value,) + others)[0]


def place(bit):
    return (lax.axis_index("dom") // bit) % 2


def core_and_line():
    sub = lax.axis_index("sub")
    return sub % 2, sub // 2


def bytes_of(shapes):
    return sum(math.prod(s.shape) * s.dtype.itemsize for s in shapes)


def call(
    kernel, out_shape, flops, *operands, far=(), far_out=(), near_out=(), scratch=(), vmem=6, alias=None
):
    several = isinstance(out_shape, list)
    outs = out_shape if several else [out_shape]

    def specs(count, away):
        return [
            pl.BlockSpec(memory_space=pltpu.HBM if i in away else pltpu.VMEM) for i in range(count)
        ]

    out_specs = specs(len(outs), far_out)
    results = list(outs)
    for i in far_out:
        results[i] = pltpu.HBM(outs[i].shape, outs[i].dtype)
    for i in near_out:
        results[i] = pltpu.VMEM(outs[i].shape, outs[i].dtype)
    operands = [
        pltpu.with_memory_space_constraint(x, pltpu.HBM) if i in far else x
        for i, x in enumerate(operands)
    ]
    return pl.pallas_call(
        kernel,
        in_specs=specs(len(operands), far),
        out_specs=out_specs if several else out_specs[0],
        out_shape=results if several else results[0],
        scratch_shapes=scratch,
        input_output_aliases=alias or {},
        compiler_params=pltpu.CompilerParams(vmem_limit_bytes=vmem * 2**20),
        cost_estimate=pl.CostEstimate(
            flops=1, bytes_accessed=1, transcendentals=0
        ),
    )(*operands)


def struct(shape, dtype=jnp.float32):
    return jax.ShapeDtypeStruct(shape, dtype)


def dot(a, b, dims=(((1,), (0,)), ((), ()))):
    return lax.dot_general(a, b, dims, preferred_element_type=jnp.float32)


def tiles(length, width, body):
    def step(i, carry):
        body(i, pl.ds(pl.multiple_of(i * width, width), width))
        return carry

    lax.fori_loop(0, length // width, step, 0)


def column_tiles(array, width):
    return [array.at[:, pl.ds(j * width, width)] for j in range(array.shape[1] // width)]


def picked(routes, rows):
    devices, slots = routes.shape
    halo = devices * slots
    slot_of = lax.broadcasted_iota(jnp.int32, (slots, halo), 1) % slots
    spread = (slot_of == lax.broadcasted_iota(jnp.int32, (slots, halo), 0)).astype(jnp.bfloat16)
    by_device = dot(routes[...].astype(jnp.float32).astype(jnp.bfloat16), spread)
    device_of = lax.broadcasted_iota(jnp.int32, (devices, halo), 1) // slots
    here = device_of == lax.broadcasted_iota(jnp.int32, (devices, halo), 0)
    wanted = jnp.sum(jnp.where(here, by_device, 0.0), 0, keepdims=True).astype(jnp.int32)
    return (wanted == lax.broadcasted_iota(jnp.int32, (rows, halo), 0)).astype(jnp.bfloat16)


def pick_kernel(send_rows, features, out, routes, features_here, out_here, reach, arrive, leave):
    inward = [
        pltpu.make_async_copy(*refs, arrive.at[j])
        for j, refs in enumerate(
            zip(column_tiles(features, 512), column_tiles(features_here, 512))
        )
    ]
    outward = [
        pltpu.make_async_copy(*refs, leave.at[j])
        for j, refs in enumerate(zip(column_tiles(out_here, 512), column_tiles(out, 512)))
    ]
    rows_in = pltpu.make_async_copy(send_rows, routes, reach)
    rows_in.start()
    for copy in inward:
        copy.start()
    rows_in.wait()
    pick = picked(routes, features.shape[0])
    for j, copy in enumerate(inward):
        copy.wait()
        at = slice(j * 512, (j + 1) * 512)
        out_here[:, at] = dot(pick, features_here[:, at], contract_rows).astype(jnp.bfloat16)
        outward[j].start()
    for copy in outward:
        copy.wait()


def counts_kernel(
    neighbours, degrees, valid, routes, counts_out, scale_out, mask_out, pick_out
):
    slots, rows = neighbours.shape
    table = counts_out.shape[0]
    pick_out[...] = picked(routes, rows)
    step = 64

    def lanes_to_rows(value):
        return jnp.transpose(jnp.broadcast_to(value, (128, rows)))[:, :1]

    scale_out[...] = lanes_to_rows(1.0 / (degrees[...].astype(jnp.float32) + 1.0))
    mask_out[...] = lanes_to_rows(valid[...].astype(jnp.float32))
    own = lax.broadcasted_iota(jnp.int32, (1, rows), 1)

    def body(i, carry):
        at = pl.ds(pl.multiple_of(i * step, step), step)
        entry = i * step + lax.broadcasted_iota(jnp.int32, (step, rows), 0)
        total = jnp.where(entry == own, 2.0, 0.0)
        for k in range(slots):
            used = jnp.where(degrees[...] > k, neighbours[k : k + 1], -1)
            total += jnp.where(entry == used, 1.0, 0.0)
        counts_out[at] = total.astype(jnp.bfloat16)
        return carry

    lax.fori_loop(0, table // step, body, 0)


def linear_kernel(
    counts_t,
    features,
    arrived,
    scale,
    mask,
    weight,
    mixed_out,
    line_out,
    pair_out,
    linear_out,
    stats_out,
    weight_here,
    arrive,
):
    tile = 512
    copies = [
        pltpu.make_async_copy(*refs, arrive.at[j])
        for j, refs in enumerate(zip(column_tiles(weight, tile), column_tiles(weight_here, tile)))
    ]
    for copy in copies:
        copy.start()
    rows, width = features.shape
    pieces, _, piece = mixed_out.shape
    for j in range(pieces):
        part = slice(j * piece, (j + 1) * piece)
        summed = dot(counts_t[:rows], features[:, part], contract_rows)
        summed += dot(counts_t[rows:], arrived[:, part], contract_rows)
        mixed_out[j] = (summed * scale[...]).astype(jnp.bfloat16)
    _, line = core_and_line()
    pair = place(1)
    for j in range(2):
        line_out[j] = mixed_out[2 * (1 - line) + j]
        pair_out[j] = mixed_out[2 * j + (1 - pair)]
    count = jnp.sum(mask[...])
    for i, copy in enumerate(copies):
        copy.wait()
        at = slice(i * tile, (i + 1) * tile)
        linear = dot(mixed_out[0], weight_here[:piece, at])
        for j in range(1, pieces):
            linear += dot(mixed_out[j], weight_here[j * piece : (j + 1) * piece, at])
        linear_out[:, at] = linear
        total = jnp.sum(mask[...] * linear, 0, keepdims=True)
        off = linear - total / jnp.maximum(count, 1.0)
        stats_out[0:1, at] = jnp.full_like(total, count)
        stats_out[1:2, at] = total
        stats_out[2:3, at] = jnp.sum(mask[...] * off * off, 0, keepdims=True)


def column_terms(stats):
    count = stats[0:1]
    return stats[1:2] / count, lax.rsqrt(stats[2:3] / count + epsilon), count


def gelu_kernel(
    linear, stats, gain, shift, cotangent, mask, active, slope_out, sums_out, active_here, leave
):
    rows, width = linear.shape
    root, cubic = 0.7978845608028654, 0.044715

    def copy(at):
        return pltpu.make_async_copy(active_here.at[:, at], active.at[:, at], leave)

    def body(i, at):
        mean, inverse, _ = column_terms(stats[:, at])
        first = second = 0.0
        for r in range(0, rows, 64):
            here = slice(r, r + 64)
            normed = (linear[here, at] - mean) * inverse
            value = gain[:, at] * normed + shift[:, at]
            square = value * value
            bent = jnp.tanh(root * value * (1.0 + cubic * square))
            upper = 0.5 * (1.0 + bent)
            active_here[here, at] = (mask[here] * (value * upper)).astype(jnp.bfloat16)
            inner = 0.5 * root * value * (1.0 - bent * bent) * (1.0 + 3.0 * cubic * square)
            slope = mask[here] * cotangent[here, at].astype(jnp.float32) * (upper + inner)
            slope_out[here, at] = slope
            first = first + jnp.sum(slope * normed, 0, keepdims=True)
            second = second + jnp.sum(slope, 0, keepdims=True)
        sums_out[0:1, at] = first
        sums_out[1:2, at] = second
        copy(at).start()

    tiles(width, 256, body)
    pltpu.make_async_copy(active_here, active, leave).wait()


def grad_kernel(linear, stats, sums, gain, slope, mask, grad_out, gain_out, shift_out, *near):
    rows, width = linear.shape
    pieces, _, piece = grad_out.shape
    gain_out[...] = sums[0:1]
    shift_out[...] = sums[1:2]

    def body(i, at):
        mean, inverse, count = column_terms(stats[:, at])
        factor = gain[:, at] * inverse
        along, offset = sums[0:1, at] / count, sums[1:2, at] / count
        for r in range(0, rows, 32):
            here = slice(r, r + 32)
            normed = (linear[here, at] - mean) * inverse
            grad_out[i, here] = (
                mask[here] * factor * (slope[here, at] - (offset + normed * along))
            ).astype(jnp.bfloat16)

    tiles(width, piece, body)
    core, _ = core_and_line()
    for k, out in enumerate(near):
        flow, chunk = divmod(k, splits)
        part = out.shape[1] // 2
        first = sum(chunk_widths[:chunk])
        at = slice(first, first + part)
        out[:, :part] = grad_out[2 * core + flow, :, at]
        out[:, part:] = grad_out[2 * (1 - core) + flow, :, at]


def back_kernel(grad, weight, counts_t, scale, own, halo, own_here, halo_here, leave):
    pieces, rows, piece = grad.shape
    tile = 512
    outward = []
    for i in range(weight.shape[0] // tile):
        at = slice(i * tile, (i + 1) * tile)
        total = dot(grad[0], weight[at, :piece], contract_columns)
        for b in range(1, pieces):
            total += dot(grad[b], weight[at, b * piece : (b + 1) * piece], contract_columns)
        weighted = (total * scale[...]).astype(jnp.bfloat16)
        halo_here[:, at] = dot(counts_t[rows:], weighted).astype(jnp.bfloat16)
        own_here[:, at] = dot(counts_t[:rows], weighted)
        for k, refs in enumerate(((halo_here, halo), (own_here, own))):
            source, target = (ref.at[:, pl.ds(i * tile, tile)] for ref in refs)
            outward.append(pltpu.make_async_copy(source, target, leave.at[2 * i + k]))
            outward[-1].start()
    for copy in outward:
        copy.wait()


def last_kernel(own, pick_t, returned, out, here, arrive, leave):
    inward = [
        pltpu.make_async_copy(*refs, arrive.at[j])
        for j, refs in enumerate(zip(column_tiles(own, 512), column_tiles(here, 512)))
    ]
    outward = [
        pltpu.make_async_copy(*refs, leave.at[j])
        for j, refs in enumerate(zip(column_tiles(here, 512), column_tiles(out, 512)))
    ]
    for copy in inward:
        copy.start()
    for j, copy in enumerate(inward):
        at = slice(j * 512, (j + 1) * 512)
        came = dot(pick_t[...], returned[:, at])
        copy.wait()
        here[:, at] += came
        outward[j].start()
    for copy in outward:
        copy.wait()


def product_kernel(flow, own, far, grad, grad_far, send_out, keep_out):
    _, line = core_and_line()
    mine = (place(1), line)[flow]
    width = keep_out.shape[2]
    for k, which in enumerate((1 - mine, mine)):
        near = (2 * line + which, 2 * which + place(1))[flow]
        total = dot(own[near], grad[...], contract_rows)
        total += dot(far[which], grad_far[...], contract_rows)
        keep_out[k] = total[:, :width]
        send_out[k] = total[:, width:].astype(jnp.bfloat16)


def cores_kernel(keep, got, send_out, keep_out):
    send_out[...] = (keep[0] + got[0].astype(jnp.float32)).astype(jnp.bfloat16)
    keep_out[...] = keep[1] + got[1].astype(jnp.float32)


def split_kernel(bit, keep, got, send_out, keep_out):
    rows = keep_out.shape[0]
    mine = place(bit)
    for which, out in ((1 - mine, send_out), (mine, keep_out)):
        at = pl.ds(pl.multiple_of(which * rows, rows), rows)
        out[...] = (keep[at] + got[at].astype(jnp.float32)).astype(out.dtype)


def add_kernel(keep, got, out):
    out[...] = (keep[...].astype(jnp.float32) + got[...].astype(jnp.float32)).astype(out.dtype)


def join_kernel(bit, own, got, out):
    rows = own.shape[0]
    mine = place(bit)
    out[pl.ds(pl.multiple_of(mine * rows, rows), rows)] = own[...]
    out[pl.ds(pl.multiple_of((1 - mine) * rows, rows), rows)] = got[...]


def stack_kernel(own, got, out):
    out[0] = own[...]
    out[1] = got[...]


def sort_kernel(bit, own_first, got_first, own_second, got_second, send_out, keep_out):
    core, _ = core_and_line()
    pair, mine = place(1), place(bit)
    rows, width = own_first.shape
    part = rows // 2
    for block, out in ((1 - core, send_out), (core, keep_out)):
        own_block = block == pair

        @pl.when(own_block)
        def _():
            out[:, :width] = own_first[...]

        @pl.when(jnp.logical_not(own_block))
        def _():
            out[:, :width] = got_first[...]

        which = jnp.where(own_block, 0, 1)
        out[pl.ds(pl.multiple_of(mine * part, part), part), width:] = own_second[which]
        out[pl.ds(pl.multiple_of((1 - mine) * part, part), part), width:] = got_second[which]


def place_kernel(own, *refs):
    parts, (out, wide, leave) = refs[:splits], refs[-3:]
    core, _ = core_and_line()
    half = core if own else 1 - core
    rows, piece = parts[0].shape[0], sum(chunk_widths)
    height = rows // 2
    copies = []
    for j in range(2):
        here = pl.ds(j * height, height)
        for flow in (0, 1):
            for chunk, width in enumerate(chunk_widths):
                first = flow * piece + sum(chunk_widths[:chunk])
                at = pl.ds(first, width)
                wide[here, at] = parts[chunk][here, pl.ds(flow * width, width)].astype(jnp.float32)
                column = pl.multiple_of(half * 2 * piece + first, 128)
                target = out.at[here, pl.ds(column, width)]
                copies.append(pltpu.make_async_copy(wide.at[here, at], target, leave.at[len(copies)]))
                copies[-1].start()
    for copy in copies:
        copy.wait()


kernel_waits = {(1, 1): [(0, 0, 0), (0, 1, 0)], (1, 3): [(3, 1, 0)]}
swap_waits = {}


class WeightGradient:
    def __init__(self, mixed, to_share):
        self.mixed, self.far = mixed, list(to_share)
        _, self.rows, self.piece = mixed.shape
        self.ended, self.summed = {}, {}

    def over(self, flow, value):
        return swap(value, "sub", 2) if flow == 0 else swap(value, "dom", 1)

    def share(self, flow, start):
        self.far[flow] = self.over(flow, after(self.far[flow], start))

    def ordered(self, step, flow, chunk, value, move):
        keys = swap_waits.get((chunk, step), ())
        value = after(value, *(self.ended[key] for key in keys if key in self.ended))
        value = move(value)
        self.ended[step, flow, chunk] = value
        return value

    def gate(self, step, chunk, value, flow):
        return after(value, *(self.ended[key] for key in kernel_waits.get((chunk, step), ()) if key in self.ended))

    def spread(self, flow, chunk):
        near = self.near[flow * splits + chunk]
        self.grad_far[flow, chunk] = self.ordered(0, flow, chunk, near, functools.partial(self.over, flow))

    def product(self, flow, chunk, gate):
        piece, rows = self.piece, self.rows
        far = self.grad_far[flow, chunk]
        width = far.shape[1] // 2
        send, keep = call(
            functools.partial(product_kernel, flow),
            [struct((2, piece, width), jnp.bfloat16), struct((2, piece, width))],
            16 * rows * piece * width,
            self.mixed,
            self.far[flow],
            self.near[flow * splits + chunk],
            after(far, gate) if gate is not None else far,
        )
        send, keep = call(
            cores_kernel,
            [struct((piece, width), jnp.bfloat16), struct((piece, width))],
            piece * width,
            keep,
            swap(send, "sub", 1),
        )
        self.summed.setdefault(chunk, []).append(send)
        return send, keep

    def chunk_steps(self, chunk, gate):
        bits = [1 << k for k in range(lax.axis_size("dom").bit_length() - 1)]
        rest = bits[1:]
        flows = (0, 1)
        step = 0

        def move(flow, value, axis, bit):
            return self.ordered(step, flow, chunk, value, lambda v: swap(v, axis, bit))

        for flow in flows:
            self.spread(flow, chunk)
        yield
        step += 1
        sends, parts = zip(*[self.product(flow, chunk, gate) for flow in flows])
        links = (("dom", 1), ("sub", 2))
        gots = [move(flow, sends[flow], *links[flow]) for flow in flows]
        parts = list(parts)
        yield
        for bit in rest[:-1]:
            step += 1
            for flow in flows:
                rows, width = parts[flow].shape
                send, parts[flow] = call(
                    functools.partial(split_kernel, bit),
                    [struct((rows // 2, width), jnp.bfloat16), struct((rows // 2, width))],
                    rows * width,
                    self.gate(step, chunk, parts[flow], flow),
                    gots[flow],
                )
                gots[flow] = move(flow, send, "dom", bit)
            yield
        step += 1
        for flow in flows:
            shape = struct(parts[flow].shape, jnp.bfloat16)
            kept = self.gate(step, chunk, parts[flow], flow)
            parts[flow] = call(add_kernel, shape, 1000, kept, gots[flow])
            gots[flow] = move(flow, parts[flow], "dom", rest[-1])
        yield
        for flow in flows:
            shape = struct(parts[flow].shape, jnp.bfloat16)
            kept = self.gate(step + 1, chunk, parts[flow], flow)
            parts[flow] = call(add_kernel, shape, 1000, kept, gots[flow])

        def join(part, flow, bit):
            rows, width = part.shape
            return call(
                functools.partial(join_kernel, bit),
                struct((2 * rows, width), jnp.bfloat16),
                rows * width,
                part,
                move(flow, part, "dom", bit),
            )

        first, second = parts
        for bit in reversed(rest[1:-1]):
            step += 1
            first, second = join(first, 0, bit), join(second, 1, bit)
            yield
        step += 1
        first = join(first, 0, rest[0])
        second = call(
            stack_kernel,
            struct((2,) + second.shape, jnp.bfloat16),
            second.size,
            second,
            move(1, second, "dom", 1),
        )
        yield
        step += 1
        first_got = move(0, first, "dom", 1)
        second_got = move(1, second, "dom", rest[0])
        yield
        if self.features is None:
            self.features = self.features_out(second)
        rows, width = first.shape
        send, keep = call(
            functools.partial(sort_kernel, rest[0]),
            [struct((rows, 2 * width), jnp.bfloat16)] * 2,
            rows * width,
            after(first, self.features),
            first_got,
            second,
            second_got,
        )
        other = swap(send, "sub", 1)
        self.results[chunk] = keep, other

    def finish(self, gate, features_out, send_back):
        self.results, self.features_out, self.features, self.out = {}, features_out, None, None
        chunks = [self.chunk_steps(chunk, gate) for chunk in range(splits)]
        tick, running = 0, set(range(splits))
        while running:
            for chunk in sorted(running):
                if tick >= chunk * lag:
                    try:
                        next(chunks[chunk])
                    except StopIteration:
                        running.discard(chunk)
            if tick == 1:
                send_back(self.ended[0, 0, 0], self.ended[0, 1, 0])
            tick += 1
        out = None
        for own in (True, False):
            out = self.place(own, [self.results[chunk][1 - own] for chunk in range(splits)], out)
        return out, self.features

    def place(self, own, parts, out):
        rows, width = parts[0].shape[0], 2 * sum(chunk_widths)
        into = {} if out is None else dict(far=(splits,), alias={splits: 0})
        return call(
            functools.partial(place_kernel, own),
            struct((rows, 2 * width)),
            1,
            *parts,
            *([] if out is None else [out]),
            far_out=(0,),
            scratch=[
                pltpu.VMEM((rows, width), jnp.float32),
                pltpu.SemaphoreType.DMA((4 * splits,)),
            ],
            **into,
        )


def on_device(
    features, weight, bn_gain, bn_shift, cotangent, neighbours, degrees, send_rows, valid_nodes
):
    rows, width = features.shape
    halo = send_rows.size
    devices = lax.axis_size("dom") * lax.axis_size("sub")
    piece = width // 4

    def to_all(value):
        value = value.reshape(devices, halo // devices, width)
        return lax.all_to_all(value, both_axes, 0, 0, tiled=True).reshape(halo, width)

    routes = send_rows.reshape(devices, halo // devices)
    outgoing = call(
        pick_kernel,
        struct((halo, width), jnp.bfloat16),
        2 * halo * rows * width,
        routes,
        features,
        far=(0, 1),
        far_out=(0,),
        scratch=[
            pltpu.VMEM(routes.shape, jnp.int32),
            pltpu.VMEM((rows, width), jnp.bfloat16),
            pltpu.VMEM((halo, width), jnp.bfloat16),
            pltpu.SemaphoreType.DMA,
            pltpu.SemaphoreType.DMA((width // 512,)),
            pltpu.SemaphoreType.DMA((width // 512,)),
        ],
        vmem=6 + (halo * width >> 19),
    )
    arrived = to_all(outgoing)
    gain, shift = bn_gain[None, :], bn_shift[None, :]
    counts_t, scale, mask, pick_t = call(
        counts_kernel,
        [
            struct((rows + halo, rows), jnp.bfloat16),
            struct((rows, 1)),
            struct((rows, 1)),
            struct((rows, halo), jnp.bfloat16),
        ],
        3 * neighbours.size * (rows + halo),
        neighbours.T,
        degrees[None, :],
        valid_nodes[None, :],
        routes,
    )

    share = struct((2, rows, piece), jnp.bfloat16)
    mixed, *to_share, linear, stats, weight_here = call(
        linear_kernel,
        [
            struct((4, rows, piece), jnp.bfloat16),
            share,
            share,
            struct((rows, width)),
            struct((3, width)),
            struct(weight.shape, jnp.bfloat16),
        ],
        2 * rows * width * (width + rows + halo),
        counts_t,
        features,
        arrived,
        scale,
        mask,
        weight,
        far=(5,),
        near_out=(5,),
        scratch=[pltpu.SemaphoreType.DMA((width // 512,))],
    )

    product = WeightGradient(mixed, to_share)
    stats, merged = merge_statistics(stats)
    for flow in (0, 1):
        product.share(flow, merged[flow])

    active, slope, sums = call(
        gelu_kernel,
        [struct((rows, width), jnp.bfloat16), struct((rows, width)), struct((2, width))],
        40 * rows * width,
        linear,
        stats,
        gain,
        shift,
        cotangent,
        mask,
        far_out=(0,),
        scratch=[pltpu.VMEM((rows, width), jnp.bfloat16), pltpu.SemaphoreType.DMA],
    )
    sums, *product.far = lax.optimization_barrier((sums, *product.far))
    sums = sum_over_all(sums)

    grad, grad_gain, grad_shift, *near = call(
        grad_kernel,
        [struct((4, rows, piece), jnp.bfloat16), struct((1, width)), struct((1, width))]
        + [struct((rows, 2 * wide), jnp.bfloat16) for wide in chunk_widths] * 2,
        10 * rows * width,
        linear,
        stats,
        sums,
        gain,
        slope,
        mask,
    )
    product.near, product.grad_far = near, {}
    own_grad, halo_grad = call(
        back_kernel,
        [struct((rows, width)), struct((halo, width), jnp.bfloat16)],
        2 * rows * width * (width + rows + halo),
        grad,
        weight_here,
        counts_t,
        scale,
        far_out=(0, 1),
        scratch=[
            pltpu.VMEM((rows, width), jnp.float32),
            pltpu.VMEM((halo, width), jnp.bfloat16),
            pltpu.SemaphoreType.DMA((2 * width // 512,)),
        ],
        vmem=6 + (halo * width >> 19),
    )

    def send_back(*start):
        product.returned = to_all(after(halo_grad, *start))

    def features_out(start):
        return call(
            last_kernel,
            struct((rows, width)),
            2 * rows * width * halo,
            own_grad,
            pick_t,
            after(product.returned, start),
            far=(0,),
            far_out=(0,),
            scratch=[
                pltpu.VMEM((rows, width), jnp.float32),
                pltpu.SemaphoreType.DMA((width // 512,)),
                pltpu.SemaphoreType.DMA((width // 512,)),
            ],
        )

    grad_weight, grad_features = product.finish(halo_grad, features_out, send_back)
    return (active, grad_features, grad_weight, grad_gain[0], grad_shift[0])


def solution(mesh):
    return jax.shard_map(
        on_device,
        mesh=mesh,
        in_specs=(
            P(("dom", "sub"), None),
            P(),
            P(),
            P(),
            P(("dom", "sub"), None),
            P(("dom", "sub"), None),
            P(("dom", "sub")),
            P(("dom", "sub"), None, None, None),
            P(("dom", "sub")),
        ),
        out_specs=(P(("dom", "sub"), None), P(("dom", "sub"), None), P("sub", None), P(), P()),
        check_vma=False,
    )
```

```python
import functools
import math

import jax
import jax.numpy as jnp
from jax import lax
from jax.experimental import pallas as pl
from jax.experimental.pallas import tpu as pltpu
from jax.sharding import PartitionSpec as P

epsilon = 1e-05
chunk_widths = (256, 256)
splits = len(chunk_widths)
lag = 1
both_axes = ("dom", "sub")
contract_rows = (((0,), (0,)), ((), ()))
contract_columns = (((1,), (1,)), ((), ()))


def swap(value, axis, offset):
    size = lax.axis_size(axis)
    return lax.ppermute(value, axis, [(i, i ^ offset) for i in range(size)])


def tree_sum(terms):
    while len(terms) > 1:
        terms = [terms[i] + terms[i + 1] for i in range(0, len(terms), 2)]
    return terms[0]


def exchange_steps():
    steps = []
    for axis in ("sub", "dom"):
        size, low = lax.axis_size(axis), 1
        odd = (size.bit_length() - 1) % 2
        while low < size:
            width = 2 if odd else 4
            odd = 0
            steps.append((axis, [low * k for k in range(1, width)]))
            low *= width
    return steps


def sum_over_all(value, other):
    for step, (axis, offsets) in enumerate(exchange_steps()):
        if step == 1:
            value, other = lax.optimization_barrier((value, other))
        value = tree_sum([value] + [swap(value, axis, offset) for offset in offsets])
    return value, other


def merge_kernel(*refs):
    *parts, out = refs
    parts = [(p[0:1], p[1:2], p[2:3]) for p in parts]
    count = tree_sum([p[0] for p in parts])
    total = tree_sum([p[1] for p in parts])
    mean = total / jnp.maximum(count, 1.0)
    out[0:1] = count
    out[1:2] = total
    out[2:3] = tree_sum([p[2] + p[0] * jnp.square(p[1] / jnp.maximum(p[0], 1.0) - mean) for p in parts])


def merge_statistics(packed):
    steps = []
    for axis, offsets in exchange_steps():
        parts = [packed] + [swap(packed, axis, offset) for offset in offsets]
        packed = call(merge_kernel, struct(packed.shape), 30 * packed.size, *parts)
        steps.append(packed)
    return packed, steps


def after(value, *others):
    return lax.optimization_barrier((value,) + others)[0]


def place(bit):
    return (lax.axis_index("dom") // bit) % 2


def core_and_line():
    sub = lax.axis_index("sub")
    return sub % 2, sub // 2


def bytes_of(shapes):
    return sum(math.prod(s.shape) * s.dtype.itemsize for s in shapes)


def call(
    kernel, out_shape, flops, *operands, far=(), far_out=(), near_out=(), scratch=(), vmem=6, alias=None
):
    several = isinstance(out_shape, list)
    outs = out_shape if several else [out_shape]

    def specs(count, away):
        return [
            pl.BlockSpec(memory_space=pltpu.HBM if i in away else pltpu.VMEM) for i in range(count)
        ]

    out_specs = specs(len(outs), far_out)
    results = list(outs)
    for i in far_out:
        results[i] = pltpu.HBM(outs[i].shape, outs[i].dtype)
    for i in near_out:
        results[i] = pltpu.VMEM(outs[i].shape, outs[i].dtype)
    operands = [
        pltpu.with_memory_space_constraint(x, pltpu.HBM) if i in far else x
        for i, x in enumerate(operands)
    ]
    return pl.pallas_call(
        kernel,
        in_specs=specs(len(operands), far),
        out_specs=out_specs if several else out_specs[0],
        out_shape=results if several else results[0],
        scratch_shapes=scratch,
        input_output_aliases=alias or {},
        compiler_params=pltpu.CompilerParams(vmem_limit_bytes=vmem * 2**20),
        cost_estimate=pl.CostEstimate(
            flops=1, bytes_accessed=1, transcendentals=0
        ),
    )(*operands)


def struct(shape, dtype=jnp.float32):
    return jax.ShapeDtypeStruct(shape, dtype)


def dot(a, b, dims=(((1,), (0,)), ((), ()))):
    return lax.dot_general(a, b, dims, preferred_element_type=jnp.float32)


def tiles(length, width, body):
    def step(i, carry):
        body(i, pl.ds(pl.multiple_of(i * width, width), width))
        return carry

    lax.fori_loop(0, length // width, step, 0)


def column_tiles(array, width):
    return [array.at[:, pl.ds(j * width, width)] for j in range(array.shape[1] // width)]


def picked(routes, rows):
    devices, slots = routes.shape
    halo = devices * slots
    slot_of = lax.broadcasted_iota(jnp.int32, (slots, halo), 1) % slots
    spread = (slot_of == lax.broadcasted_iota(jnp.int32, (slots, halo), 0)).astype(jnp.bfloat16)
    by_device = dot(routes[...].astype(jnp.float32).astype(jnp.bfloat16), spread)
    device_of = lax.broadcasted_iota(jnp.int32, (devices, halo), 1) // slots
    here = device_of == lax.broadcasted_iota(jnp.int32, (devices, halo), 0)
    wanted = jnp.sum(jnp.where(here, by_device, 0.0), 0, keepdims=True).astype(jnp.int32)
    return (wanted == lax.broadcasted_iota(jnp.int32, (rows, halo), 0)).astype(jnp.bfloat16)


def pick_kernel(send_rows, features, out, routes, features_here, out_here, reach, arrive, leave):
    inward = [
        pltpu.make_async_copy(*refs, arrive.at[j])
        for j, refs in enumerate(
            zip(column_tiles(features, 512), column_tiles(features_here, 512))
        )
    ]
    outward = [
        pltpu.make_async_copy(*refs, leave.at[j])
        for j, refs in enumerate(zip(column_tiles(out_here, 512), column_tiles(out, 512)))
    ]
    rows_in = pltpu.make_async_copy(send_rows, routes, reach)
    rows_in.start()
    for copy in inward:
        copy.start()
    rows_in.wait()
    pick = picked(routes, features.shape[0])
    for j, copy in enumerate(inward):
        copy.wait()
        at = slice(j * 512, (j + 1) * 512)
        out_here[:, at] = dot(pick, features_here[:, at], contract_rows).astype(jnp.bfloat16)
        outward[j].start()
    for copy in outward:
        copy.wait()


def counts_kernel(
    neighbours, degrees, valid, routes, counts_out, scale_out, mask_out, pick_out
):
    slots, rows = neighbours.shape
    table = counts_out.shape[0]
    pick_out[...] = picked(routes, rows)
    step = 64

    def lanes_to_rows(value):
        return jnp.transpose(jnp.broadcast_to(value, (128, rows)))[:, :1]

    scale_out[...] = lanes_to_rows(1.0 / (degrees[...].astype(jnp.float32) + 1.0))
    mask_out[...] = lanes_to_rows(valid[...].astype(jnp.float32))
    own = lax.broadcasted_iota(jnp.int32, (1, rows), 1)

    def body(i, carry):
        at = pl.ds(pl.multiple_of(i * step, step), step)
        entry = i * step + lax.broadcasted_iota(jnp.int32, (step, rows), 0)
        total = jnp.where(entry == own, 2.0, 0.0)
        for k in range(slots):
            used = jnp.where(degrees[...] > k, neighbours[k : k + 1], -1)
            total += jnp.where(entry == used, 1.0, 0.0)
        counts_out[at] = total.astype(jnp.bfloat16)
        return carry

    lax.fori_loop(0, table // step, body, 0)


def linear_kernel(
    counts_t,
    features,
    arrived,
    scale,
    mask,
    weight,
    mixed_out,
    line_out,
    pair_out,
    linear_out,
    stats_out,
    weight_here,
    arrive,
):
    tile = 512
    copies = [
        pltpu.make_async_copy(*refs, arrive.at[j])
        for j, refs in enumerate(zip(column_tiles(weight, tile), column_tiles(weight_here, tile)))
    ]
    for copy in copies:
        copy.start()
    rows, width = features.shape
    pieces, _, piece = mixed_out.shape
    for j in range(pieces):
        part = slice(j * piece, (j + 1) * piece)
        summed = dot(counts_t[:rows], features[:, part], contract_rows)
        summed += dot(counts_t[rows:], arrived[:, part], contract_rows)
        mixed_out[j] = (summed * scale[...]).astype(jnp.bfloat16)
    _, line = core_and_line()
    pair = place(1)
    for j in range(2):
        line_out[j] = mixed_out[2 * (1 - line) + j]
        pair_out[j] = mixed_out[2 * j + (1 - pair)]
    count = jnp.sum(mask[...])
    for i, copy in enumerate(copies):
        copy.wait()
        at = slice(i * tile, (i + 1) * tile)
        linear = dot(mixed_out[0], weight_here[:piece, at])
        for j in range(1, pieces):
            linear += dot(mixed_out[j], weight_here[j * piece : (j + 1) * piece, at])
        linear_out[:, at] = linear
        total = jnp.sum(mask[...] * linear, 0, keepdims=True)
        off = linear - total / jnp.maximum(count, 1.0)
        stats_out[0:1, at] = jnp.full_like(total, count)
        stats_out[1:2, at] = total
        stats_out[2:3, at] = jnp.sum(mask[...] * off * off, 0, keepdims=True)


def column_terms(stats):
    count = stats[0:1]
    return stats[1:2] / count, lax.rsqrt(stats[2:3] / count + epsilon), count


def gelu_kernel(
    linear, stats, gain, shift, cotangent, mask, active, slope_out, sums_out, active_here, leave
):
    rows, width = linear.shape
    root, cubic = 0.7978845608028654, 0.044715

    def copy(at):
        return pltpu.make_async_copy(active_here.at[:, at], active.at[:, at], leave)

    def body(i, at):
        mean, inverse, _ = column_terms(stats[:, at])
        first = second = 0.0
        for r in range(0, rows, 64):
            here = slice(r, r + 64)
            normed = (linear[here, at] - mean) * inverse
            value = gain[:, at] * normed + shift[:, at]
            square = value * value
            bent = jnp.tanh(root * value * (1.0 + cubic * square))
            upper = 0.5 * (1.0 + bent)
            active_here[here, at] = (mask[here] * (value * upper)).astype(jnp.bfloat16)
            inner = 0.5 * root * value * (1.0 - bent * bent) * (1.0 + 3.0 * cubic * square)
            slope = mask[here] * cotangent[here, at].astype(jnp.float32) * (upper + inner)
            slope_out[here, at] = slope
            first = first + jnp.sum(slope * normed, 0, keepdims=True)
            second = second + jnp.sum(slope, 0, keepdims=True)
        sums_out[0:1, at] = first
        sums_out[1:2, at] = second
        copy(at).start()

    tiles(width, 256, body)
    pltpu.make_async_copy(active_here, active, leave).wait()


def grad_kernel(linear, stats, sums, gain, slope, mask, grad_out, gain_out, shift_out, *near):
    rows, width = linear.shape
    pieces, _, piece = grad_out.shape
    gain_out[...] = sums[0:1]
    shift_out[...] = sums[1:2]

    def body(i, at):
        mean, inverse, count = column_terms(stats[:, at])
        factor = gain[:, at] * inverse
        along, offset = sums[0:1, at] / count, sums[1:2, at] / count
        for r in range(0, rows, 32):
            here = slice(r, r + 32)
            normed = (linear[here, at] - mean) * inverse
            grad_out[i, here] = (
                mask[here] * factor * (slope[here, at] - (offset + normed * along))
            ).astype(jnp.bfloat16)

    tiles(width, piece, body)
    core, _ = core_and_line()
    for k, out in enumerate(near):
        flow, chunk = divmod(k, splits)
        part = out.shape[1] // 2
        first = sum(chunk_widths[:chunk])
        at = slice(first, first + part)
        out[:, :part] = grad_out[2 * core + flow, :, at]
        out[:, part:] = grad_out[2 * (1 - core) + flow, :, at]


def back_kernel(grad, weight, counts_t, scale, own, halo, own_here, halo_here, leave):
    pieces, rows, piece = grad.shape
    tile = 1024
    outward = []
    for i in range(weight.shape[0] // tile):
        at = slice(i * tile, (i + 1) * tile)
        total = dot(grad[0], weight[at, :piece], contract_columns)
        for b in range(1, pieces):
            total += dot(grad[b], weight[at, b * piece : (b + 1) * piece], contract_columns)
        weighted = (total * scale[...]).astype(jnp.bfloat16)
        halo_here[:, at] = dot(counts_t[rows:], weighted).astype(jnp.bfloat16)
        own_here[:, at] = dot(counts_t[:rows], weighted)
        for k, refs in enumerate(((halo_here, halo), (own_here, own))):
            source, target = (ref.at[:, pl.ds(i * tile, tile)] for ref in refs)
            outward.append(pltpu.make_async_copy(source, target, leave.at[2 * i + k]))
            outward[-1].start()
    for copy in outward:
        copy.wait()


def last_kernel(own, pick_t, returned, out, here, arrive, leave):
    inward = [
        pltpu.make_async_copy(*refs, arrive.at[j])
        for j, refs in enumerate(zip(column_tiles(own, 512), column_tiles(here, 512)))
    ]
    outward = [
        pltpu.make_async_copy(*refs, leave.at[j])
        for j, refs in enumerate(zip(column_tiles(here, 512), column_tiles(out, 512)))
    ]
    for copy in inward:
        copy.start()
    for j, copy in enumerate(inward):
        at = slice(j * 512, (j + 1) * 512)
        came = dot(pick_t[...], returned[:, at])
        copy.wait()
        here[:, at] += came
        outward[j].start()
    for copy in outward:
        copy.wait()


def product_kernel(flow, own, far, grad, grad_far, send_out, keep_out):
    _, line = core_and_line()
    mine = (place(1), line)[flow]
    width = keep_out.shape[2]
    for k, which in enumerate((1 - mine, mine)):
        near = (2 * line + which, 2 * which + place(1))[flow]
        total = dot(own[near], grad[...], contract_rows)
        total += dot(far[which], grad_far[...], contract_rows)
        keep_out[k] = total[:, :width]
        send_out[k] = total[:, width:].astype(jnp.bfloat16)


def cores_kernel(keep, got, send_out, keep_out):
    send_out[...] = (keep[0] + got[0].astype(jnp.float32)).astype(jnp.bfloat16)
    keep_out[...] = keep[1] + got[1].astype(jnp.float32)


def split_kernel(bit, keep, got, send_out, keep_out):
    rows = keep_out.shape[0]
    mine = place(bit)
    for which, out in ((1 - mine, send_out), (mine, keep_out)):
        at = pl.ds(pl.multiple_of(which * rows, rows), rows)
        out[...] = (keep[at] + got[at].astype(jnp.float32)).astype(out.dtype)


def add_kernel(keep, got, out):
    out[...] = (keep[...].astype(jnp.float32) + got[...].astype(jnp.float32)).astype(out.dtype)


def join_kernel(bit, own, got, out):
    rows = own.shape[0]
    mine = place(bit)
    out[pl.ds(pl.multiple_of(mine * rows, rows), rows)] = own[...]
    out[pl.ds(pl.multiple_of((1 - mine) * rows, rows), rows)] = got[...]


def stack_kernel(own, got, out):
    out[0] = own[...]
    out[1] = got[...]


def sort_kernel(bit, own_first, got_first, own_second, got_second, send_out, keep_out):
    core, _ = core_and_line()
    pair, mine = place(1), place(bit)
    rows, width = own_first.shape
    part = rows // 2
    for block, out in ((1 - core, send_out), (core, keep_out)):
        own_block = block == pair

        @pl.when(own_block)
        def _():
            out[:, :width] = own_first[...]

        @pl.when(jnp.logical_not(own_block))
        def _():
            out[:, :width] = got_first[...]

        which = jnp.where(own_block, 0, 1)
        out[pl.ds(pl.multiple_of(mine * part, part), part), width:] = own_second[which]
        out[pl.ds(pl.multiple_of((1 - mine) * part, part), part), width:] = got_second[which]


def place_kernel(own, *refs):
    parts, (out, wide, leave) = refs[:splits], refs[-3:]
    core, _ = core_and_line()
    half = core if own else 1 - core
    rows, piece = parts[0].shape[0], sum(chunk_widths)
    height = rows // 2
    copies = []
    for j in range(2):
        here = pl.ds(j * height, height)
        for flow in (0, 1):
            for chunk, width in enumerate(chunk_widths):
                first = flow * piece + sum(chunk_widths[:chunk])
                at = pl.ds(first, width)
                wide[here, at] = parts[chunk][here, pl.ds(flow * width, width)].astype(jnp.float32)
                column = pl.multiple_of(half * 2 * piece + first, 128)
                target = out.at[here, pl.ds(column, width)]
                copies.append(pltpu.make_async_copy(wide.at[here, at], target, leave.at[len(copies)]))
                copies[-1].start()
    for copy in copies:
        copy.wait()


kernel_waits = {(1, 1): [(0, 0, 0), (0, 1, 0)], (1, 3): [(3, 0, 0), (3, 1, 0)], (1, 2): [(2, 0, 0), (2, 1, 0)]}
swap_waits = {}


class WeightGradient:
    def __init__(self, mixed, to_share):
        self.mixed, self.far = mixed, list(to_share)
        _, self.rows, self.piece = mixed.shape
        self.ended, self.summed = {}, {}

    def over(self, flow, value):
        return swap(value, "sub", 2) if flow == 0 else swap(value, "dom", 1)

    def share(self, flow, start):
        self.far[flow] = self.over(flow, after(self.far[flow], start))

    def ordered(self, step, flow, chunk, value, move):
        keys = swap_waits.get((chunk, step), ())
        value = after(value, *(self.ended[key] for key in keys if key in self.ended))
        value = move(value)
        self.ended[step, flow, chunk] = value
        return value

    def gate(self, step, chunk, value, flow):
        return after(value, *(self.ended[key] for key in kernel_waits.get((chunk, step), ()) if key in self.ended))

    def spread(self, flow, chunk):
        near = self.near[flow * splits + chunk]
        self.grad_far[flow, chunk] = self.ordered(0, flow, chunk, near, functools.partial(self.over, flow))

    def product(self, flow, chunk, gate):
        piece, rows = self.piece, self.rows
        far = self.grad_far[flow, chunk]
        width = far.shape[1] // 2
        send, keep = call(
            functools.partial(product_kernel, flow),
            [struct((2, piece, width), jnp.bfloat16), struct((2, piece, width))],
            16 * rows * piece * width,
            self.mixed,
            self.far[flow],
            self.near[flow * splits + chunk],
            after(far, gate) if gate is not None else far,
        )
        send, keep = call(
            cores_kernel,
            [struct((piece, width), jnp.bfloat16), struct((piece, width))],
            piece * width,
            keep,
            swap(send, "sub", 1),
        )
        self.summed.setdefault(chunk, []).append(send)
        return send, keep

    def chunk_steps(self, chunk, gate):
        bits = [1 << k for k in range(lax.axis_size("dom").bit_length() - 1)]
        rest = bits[1:]
        flows = (0, 1)
        step = 0

        def move(flow, value, axis, bit):
            return self.ordered(step, flow, chunk, value, lambda v: swap(v, axis, bit))

        for flow in flows:
            self.spread(flow, chunk)
        yield
        step += 1
        sends, parts = zip(*[self.product(flow, chunk, gate) for flow in flows])
        links = (("dom", 1), ("sub", 2))
        gots = [move(flow, sends[flow], *links[flow]) for flow in flows]
        parts = list(parts)
        yield
        for bit in rest[:-1]:
            step += 1
            for flow in flows:
                rows, width = parts[flow].shape
                send, parts[flow] = call(
                    functools.partial(split_kernel, bit),
                    [struct((rows // 2, width), jnp.bfloat16), struct((rows // 2, width))],
                    rows * width,
                    self.gate(step, chunk, parts[flow], flow),
                    gots[flow],
                )
                gots[flow] = move(flow, send, "dom", bit)
            yield
        step += 1
        for flow in flows:
            shape = struct(parts[flow].shape, jnp.bfloat16)
            kept = self.gate(step, chunk, parts[flow], flow)
            parts[flow] = call(add_kernel, shape, 1000, kept, gots[flow])
            gots[flow] = move(flow, parts[flow], "dom", rest[-1])
        yield
        for flow in flows:
            shape = struct(parts[flow].shape, jnp.bfloat16)
            kept = self.gate(step + 1, chunk, parts[flow], flow)
            parts[flow] = call(add_kernel, shape, 1000, kept, gots[flow])

        def join(part, flow, bit):
            rows, width = part.shape
            return call(
                functools.partial(join_kernel, bit),
                struct((2 * rows, width), jnp.bfloat16),
                rows * width,
                part,
                move(flow, part, "dom", bit),
            )

        first, second = parts
        for bit in reversed(rest[1:-1]):
            step += 1
            first, second = join(first, 0, bit), join(second, 1, bit)
            yield
        step += 1
        first = join(first, 0, rest[0])
        second = call(
            stack_kernel,
            struct((2,) + second.shape, jnp.bfloat16),
            second.size,
            second,
            move(1, second, "dom", 1),
        )
        yield
        step += 1
        first_got = move(0, first, "dom", 1)
        second_got = move(1, second, "dom", rest[0])
        yield
        if self.features is None:
            self.features = self.features_out(second)
        rows, width = first.shape
        send, keep = call(
            functools.partial(sort_kernel, rest[0]),
            [struct((rows, 2 * width), jnp.bfloat16)] * 2,
            rows * width,
            after(first, self.features),
            first_got,
            second,
            second_got,
        )
        other = swap(send, "sub", 1)
        self.results[chunk] = keep, other

    def finish(self, gate, features_out, send_back):
        self.results, self.features_out, self.features, self.out = {}, features_out, None, None
        chunks = [self.chunk_steps(chunk, gate) for chunk in range(splits)]
        tick, running = 0, set(range(splits))
        while running:
            for chunk in sorted(running):
                if tick >= chunk * lag:
                    try:
                        next(chunks[chunk])
                    except StopIteration:
                        running.discard(chunk)
            if tick == 1:
                send_back(self.ended[0, 0, 0], self.ended[0, 1, 0])
            tick += 1
        out = None
        for own in (True, False):
            out = self.place(own, [self.results[chunk][1 - own] for chunk in range(splits)], out)
        return out, self.features

    def place(self, own, parts, out):
        rows, width = parts[0].shape[0], 2 * sum(chunk_widths)
        into = {} if out is None else dict(far=(splits,), alias={splits: 0})
        return call(
            functools.partial(place_kernel, own),
            struct((rows, 2 * width)),
            1,
            *parts,
            *([] if out is None else [out]),
            far_out=(0,),
            scratch=[
                pltpu.VMEM((rows, width), jnp.float32),
                pltpu.SemaphoreType.DMA((4 * splits,)),
            ],
            **into,
        )


def on_device(
    features, weight, bn_gain, bn_shift, cotangent, neighbours, degrees, send_rows, valid_nodes
):
    rows, width = features.shape
    halo = send_rows.size
    devices = lax.axis_size("dom") * lax.axis_size("sub")
    piece = width // 4

    def to_all(value):
        value = value.reshape(devices, halo // devices, width)
        return lax.all_to_all(value, both_axes, 0, 0, tiled=True).reshape(halo, width)

    routes = send_rows.reshape(devices, halo // devices)
    outgoing = call(
        pick_kernel,
        struct((halo, width), jnp.bfloat16),
        2 * halo * rows * width,
        routes,
        features,
        far=(0, 1),
        far_out=(0,),
        scratch=[
            pltpu.VMEM(routes.shape, jnp.int32),
            pltpu.VMEM((rows, width), jnp.bfloat16),
            pltpu.VMEM((halo, width), jnp.bfloat16),
            pltpu.SemaphoreType.DMA,
            pltpu.SemaphoreType.DMA((width // 512,)),
            pltpu.SemaphoreType.DMA((width // 512,)),
        ],
        vmem=6 + (halo * width >> 19),
    )
    arrived = to_all(outgoing)
    gain, shift = bn_gain[None, :], bn_shift[None, :]
    counts_t, scale, mask, pick_t = call(
        counts_kernel,
        [
            struct((rows + halo, rows), jnp.bfloat16),
            struct((rows, 1)),
            struct((rows, 1)),
            struct((rows, halo), jnp.bfloat16),
        ],
        3 * neighbours.size * (rows + halo),
        neighbours.T,
        degrees[None, :],
        valid_nodes[None, :],
        routes,
    )

    share = struct((2, rows, piece), jnp.bfloat16)
    mixed, *to_share, linear, stats, weight_here = call(
        linear_kernel,
        [
            struct((4, rows, piece), jnp.bfloat16),
            share,
            share,
            struct((rows, width)),
            struct((3, width)),
            struct(weight.shape, jnp.bfloat16),
        ],
        2 * rows * width * (width + rows + halo),
        counts_t,
        features,
        arrived,
        scale,
        mask,
        weight,
        far=(5,),
        near_out=(5,),
        scratch=[pltpu.SemaphoreType.DMA((width // 512,))],
    )

    product = WeightGradient(mixed, to_share)
    stats, merged = merge_statistics(stats)
    for flow in (0, 1):
        product.share(flow, merged[flow])

    active, slope, sums = call(
        gelu_kernel,
        [struct((rows, width), jnp.bfloat16), struct((rows, width)), struct((2, width))],
        40 * rows * width,
        linear,
        stats,
        gain,
        shift,
        cotangent,
        mask,
        far_out=(0,),
        scratch=[pltpu.VMEM((rows, width), jnp.bfloat16), pltpu.SemaphoreType.DMA],
    )
    sums, product.far[0] = lax.optimization_barrier((sums, product.far[0]))
    sums, product.far[1] = sum_over_all(sums, product.far[1])

    grad, grad_gain, grad_shift, *near = call(
        grad_kernel,
        [struct((4, rows, piece), jnp.bfloat16), struct((1, width)), struct((1, width))]
        + [struct((rows, 2 * wide), jnp.bfloat16) for wide in chunk_widths] * 2,
        10 * rows * width,
        linear,
        stats,
        sums,
        gain,
        slope,
        mask,
    )
    product.near, product.grad_far = near, {}
    own_grad, halo_grad = call(
        back_kernel,
        [struct((rows, width)), struct((halo, width), jnp.bfloat16)],
        2 * rows * width * (width + rows + halo),
        grad,
        weight_here,
        counts_t,
        scale,
        far_out=(0, 1),
        scratch=[
            pltpu.VMEM((rows, width), jnp.float32),
            pltpu.VMEM((halo, width), jnp.bfloat16),
            pltpu.SemaphoreType.DMA((2 * width // 1024,)),
        ],
        vmem=6 + (halo * width >> 19),
    )

    def send_back(*start):
        product.returned = to_all(after(halo_grad, *start))

    def features_out(start):
        return call(
            last_kernel,
            struct((rows, width)),
            2 * rows * width * halo,
            own_grad,
            pick_t,
            after(product.returned, start),
            far=(0,),
            far_out=(0,),
            scratch=[
                pltpu.VMEM((rows, width), jnp.float32),
                pltpu.SemaphoreType.DMA((width // 512,)),
                pltpu.SemaphoreType.DMA((width // 512,)),
            ],
        )

    grad_weight, grad_features = product.finish(halo_grad, features_out, send_back)
    return (active, grad_features, grad_weight, grad_gain[0], grad_shift[0])


def solution(mesh):
    return jax.shard_map(
        on_device,
        mesh=mesh,
        in_specs=(
            P(("dom", "sub"), None),
            P(),
            P(),
            P(),
            P(("dom", "sub"), None),
            P(("dom", "sub"), None),
            P(("dom", "sub")),
            P(("dom", "sub"), None, None, None),
            P(("dom", "sub")),
        ),
        out_specs=(P(("dom", "sub"), None), P(("dom", "sub"), None), P("sub", None), P(), P()),
        check_vma=False,
    )
```

```python
import functools
import math

import jax
import jax.numpy as jnp
from jax import lax
from jax.experimental import pallas as pl
from jax.experimental.pallas import tpu as pltpu
from jax.sharding import PartitionSpec as P

epsilon = 1e-05
chunk_widths = (256, 256)
splits = len(chunk_widths)
lag = 1
both_axes = ("dom", "sub")
contract_rows = (((0,), (0,)), ((), ()))
contract_columns = (((1,), (1,)), ((), ()))


def swap(value, axis, offset):
    size = lax.axis_size(axis)
    return lax.ppermute(value, axis, [(i, i ^ offset) for i in range(size)])


def tree_sum(terms):
    while len(terms) > 1:
        terms = [terms[i] + terms[i + 1] for i in range(0, len(terms), 2)]
    return terms[0]


def exchange_steps():
    steps = []
    for axis in ("sub", "dom"):
        size, low = lax.axis_size(axis), 1
        odd = (size.bit_length() - 1) % 2
        while low < size:
            width = 2 if odd else 4
            odd = 0
            steps.append((axis, [low * k for k in range(1, width)]))
            low *= width
    return steps


def sum_over_all(value, other):
    for step, (axis, offsets) in enumerate(exchange_steps()):
        if step == 1:
            value, other = lax.optimization_barrier((value, other))
        value = tree_sum([value] + [swap(value, axis, offset) for offset in offsets])
    return value, other


def merge_kernel(*refs):
    *parts, out = refs
    parts = [(p[0:1], p[1:2], p[2:3]) for p in parts]
    count = tree_sum([p[0] for p in parts])
    total = tree_sum([p[1] for p in parts])
    mean = total / jnp.maximum(count, 1.0)
    out[0:1] = count
    out[1:2] = total
    out[2:3] = tree_sum([p[2] + p[0] * jnp.square(p[1] / jnp.maximum(p[0], 1.0) - mean) for p in parts])


def merge_statistics(packed):
    steps = []
    for axis, offsets in exchange_steps():
        parts = [packed] + [swap(packed, axis, offset) for offset in offsets]
        packed = call(merge_kernel, struct(packed.shape), 30 * packed.size, *parts)
        steps.append(packed)
    return packed, steps


def after(value, *others):
    return lax.optimization_barrier((value,) + others)[0]


def place(bit):
    return (lax.axis_index("dom") // bit) % 2


def core_and_line():
    sub = lax.axis_index("sub")
    return sub % 2, sub // 2


def bytes_of(shapes):
    return sum(math.prod(s.shape) * s.dtype.itemsize for s in shapes)


def call(
    kernel, out_shape, flops, *operands, far=(), far_out=(), near_out=(), scratch=(), vmem=6, alias=None
):
    several = isinstance(out_shape, list)
    outs = out_shape if several else [out_shape]

    def specs(count, away):
        return [
            pl.BlockSpec(memory_space=pltpu.HBM if i in away else pltpu.VMEM) for i in range(count)
        ]

    out_specs = specs(len(outs), far_out)
    results = list(outs)
    for i in far_out:
        results[i] = pltpu.HBM(outs[i].shape, outs[i].dtype)
    for i in near_out:
        results[i] = pltpu.VMEM(outs[i].shape, outs[i].dtype)
    operands = [
        pltpu.with_memory_space_constraint(x, pltpu.HBM) if i in far else x
        for i, x in enumerate(operands)
    ]
    return pl.pallas_call(
        kernel,
        in_specs=specs(len(operands), far),
        out_specs=out_specs if several else out_specs[0],
        out_shape=results if several else results[0],
        scratch_shapes=scratch,
        input_output_aliases=alias or {},
        compiler_params=pltpu.CompilerParams(vmem_limit_bytes=vmem * 2**20),
        cost_estimate=pl.CostEstimate(
            flops=1, bytes_accessed=1, transcendentals=0
        ),
    )(*operands)


def struct(shape, dtype=jnp.float32):
    return jax.ShapeDtypeStruct(shape, dtype)


def dot(a, b, dims=(((1,), (0,)), ((), ()))):
    return lax.dot_general(a, b, dims, preferred_element_type=jnp.float32)


def tiles(length, width, body):
    def step(i, carry):
        body(i, pl.ds(pl.multiple_of(i * width, width), width))
        return carry

    lax.fori_loop(0, length // width, step, 0)


def column_tiles(array, width):
    return [array.at[:, pl.ds(j * width, width)] for j in range(array.shape[1] // width)]


def picked(routes, rows):
    devices, slots = routes.shape
    halo = devices * slots
    slot_of = lax.broadcasted_iota(jnp.int32, (slots, halo), 1) % slots
    spread = (slot_of == lax.broadcasted_iota(jnp.int32, (slots, halo), 0)).astype(jnp.bfloat16)
    by_device = dot(routes[...].astype(jnp.float32).astype(jnp.bfloat16), spread)
    device_of = lax.broadcasted_iota(jnp.int32, (devices, halo), 1) // slots
    here = device_of == lax.broadcasted_iota(jnp.int32, (devices, halo), 0)
    wanted = jnp.sum(jnp.where(here, by_device, 0.0), 0, keepdims=True).astype(jnp.int32)
    return (wanted == lax.broadcasted_iota(jnp.int32, (rows, halo), 0)).astype(jnp.bfloat16)


def pick_kernel(send_rows, features, out, routes, features_here, out_here, reach, arrive, leave):
    inward = [
        pltpu.make_async_copy(*refs, arrive.at[j])
        for j, refs in enumerate(
            zip(column_tiles(features, 1024), column_tiles(features_here, 1024))
        )
    ]
    outward = [
        pltpu.make_async_copy(*refs, leave.at[j])
        for j, refs in enumerate(zip(column_tiles(out_here, 1024), column_tiles(out, 1024)))
    ]
    rows_in = pltpu.make_async_copy(send_rows, routes, reach)
    rows_in.start()
    for copy in inward:
        copy.start()
    rows_in.wait()
    pick = picked(routes, features.shape[0])
    for j, copy in enumerate(inward):
        copy.wait()
        at = slice(j * 1024, (j + 1) * 1024)
        out_here[:, at] = dot(pick, features_here[:, at], contract_rows).astype(jnp.bfloat16)
        outward[j].start()
    for copy in outward:
        copy.wait()


def counts_kernel(
    neighbours, degrees, valid, routes, counts_out, scale_out, mask_out, pick_out
):
    slots, rows = neighbours.shape
    table = counts_out.shape[0]
    pick_out[...] = picked(routes, rows)
    step = 64

    def lanes_to_rows(value):
        return jnp.transpose(jnp.broadcast_to(value, (128, rows)))[:, :1]

    scale_out[...] = lanes_to_rows(1.0 / (degrees[...].astype(jnp.float32) + 1.0))
    mask_out[...] = lanes_to_rows(valid[...].astype(jnp.float32))
    own = lax.broadcasted_iota(jnp.int32, (1, rows), 1)

    def body(i, carry):
        at = pl.ds(pl.multiple_of(i * step, step), step)
        entry = i * step + lax.broadcasted_iota(jnp.int32, (step, rows), 0)
        total = jnp.where(entry == own, 2.0, 0.0)
        for k in range(slots):
            used = jnp.where(degrees[...] > k, neighbours[k : k + 1], -1)
            total += jnp.where(entry == used, 1.0, 0.0)
        counts_out[at] = total.astype(jnp.bfloat16)
        return carry

    lax.fori_loop(0, table // step, body, 0)


def linear_kernel(
    counts_t,
    features,
    arrived,
    scale,
    mask,
    weight,
    mixed_out,
    line_out,
    pair_out,
    linear_out,
    stats_out,
    weight_here,
    arrive,
):
    tile = 512
    copies = [
        pltpu.make_async_copy(*refs, arrive.at[j])
        for j, refs in enumerate(zip(column_tiles(weight, tile), column_tiles(weight_here, tile)))
    ]
    for copy in copies:
        copy.start()
    rows, width = features.shape
    pieces, _, piece = mixed_out.shape
    for j in range(pieces):
        part = slice(j * piece, (j + 1) * piece)
        summed = dot(counts_t[:rows], features[:, part], contract_rows)
        summed += dot(counts_t[rows:], arrived[:, part], contract_rows)
        mixed_out[j] = (summed * scale[...]).astype(jnp.bfloat16)
    _, line = core_and_line()
    pair = place(1)
    for j in range(2):
        line_out[j] = mixed_out[2 * (1 - line) + j]
        pair_out[j] = mixed_out[2 * j + (1 - pair)]
    count = jnp.sum(mask[...])
    for i, copy in enumerate(copies):
        copy.wait()
        at = slice(i * tile, (i + 1) * tile)
        linear = dot(mixed_out[0], weight_here[:piece, at])
        for j in range(1, pieces):
            linear += dot(mixed_out[j], weight_here[j * piece : (j + 1) * piece, at])
        linear_out[:, at] = linear
        total = jnp.sum(mask[...] * linear, 0, keepdims=True)
        off = linear - total / jnp.maximum(count, 1.0)
        stats_out[0:1, at] = jnp.full_like(total, count)
        stats_out[1:2, at] = total
        stats_out[2:3, at] = jnp.sum(mask[...] * off * off, 0, keepdims=True)


def column_terms(stats):
    count = stats[0:1]
    return stats[1:2] / count, lax.rsqrt(stats[2:3] / count + epsilon), count


def gelu_kernel(
    linear, stats, gain, shift, cotangent, mask, active, slope_out, sums_out, active_here, leave
):
    rows, width = linear.shape
    root, cubic = 0.7978845608028654, 0.044715

    def copy(at):
        return pltpu.make_async_copy(active_here.at[:, at], active.at[:, at], leave)

    def body(i, at):
        mean, inverse, _ = column_terms(stats[:, at])
        first = second = 0.0
        for r in range(0, rows, 64):
            here = slice(r, r + 64)
            normed = (linear[here, at] - mean) * inverse
            value = gain[:, at] * normed + shift[:, at]
            square = value * value
            bent = jnp.tanh(root * value * (1.0 + cubic * square))
            upper = 0.5 * (1.0 + bent)
            active_here[here, at] = (mask[here] * (value * upper)).astype(jnp.bfloat16)
            inner = 0.5 * root * value * (1.0 - bent * bent) * (1.0 + 3.0 * cubic * square)
            slope = mask[here] * cotangent[here, at].astype(jnp.float32) * (upper + inner)
            slope_out[here, at] = slope
            first = first + jnp.sum(slope * normed, 0, keepdims=True)
            second = second + jnp.sum(slope, 0, keepdims=True)
        sums_out[0:1, at] = first
        sums_out[1:2, at] = second
        copy(at).start()

    tiles(width, 256, body)
    pltpu.make_async_copy(active_here, active, leave).wait()


def grad_kernel(linear, stats, sums, gain, slope, mask, grad_out, gain_out, shift_out, *near):
    rows, width = linear.shape
    pieces, _, piece = grad_out.shape
    gain_out[...] = sums[0:1]
    shift_out[...] = sums[1:2]

    def body(i, at):
        mean, inverse, count = column_terms(stats[:, at])
        factor = gain[:, at] * inverse
        along, offset = sums[0:1, at] / count, sums[1:2, at] / count
        for r in range(0, rows, 32):
            here = slice(r, r + 32)
            normed = (linear[here, at] - mean) * inverse
            grad_out[i, here] = (
                mask[here] * factor * (slope[here, at] - (offset + normed * along))
            ).astype(jnp.bfloat16)

    tiles(width, piece, body)
    core, _ = core_and_line()
    for k, out in enumerate(near):
        flow, chunk = divmod(k, splits)
        part = out.shape[1] // 2
        first = sum(chunk_widths[:chunk])
        at = slice(first, first + part)
        out[:, :part] = grad_out[2 * core + flow, :, at]
        out[:, part:] = grad_out[2 * (1 - core) + flow, :, at]


def back_kernel(grad, weight, counts_t, scale, own, halo, own_here, halo_here, leave):
    pieces, rows, piece = grad.shape
    tile = 1024
    outward = []
    for i in range(weight.shape[0] // tile):
        at = slice(i * tile, (i + 1) * tile)
        total = dot(grad[0], weight[at, :piece], contract_columns)
        for b in range(1, pieces):
            total += dot(grad[b], weight[at, b * piece : (b + 1) * piece], contract_columns)
        weighted = (total * scale[...]).astype(jnp.bfloat16)
        halo_here[:, at] = dot(counts_t[rows:], weighted).astype(jnp.bfloat16)
        own_here[:, at] = dot(counts_t[:rows], weighted)
        for k, refs in enumerate(((halo_here, halo), (own_here, own))):
            source, target = (ref.at[:, pl.ds(i * tile, tile)] for ref in refs)
            outward.append(pltpu.make_async_copy(source, target, leave.at[2 * i + k]))
            outward[-1].start()
    for copy in outward:
        copy.wait()


def last_kernel(own, pick_t, returned, out, here, arrive, leave):
    inward = [
        pltpu.make_async_copy(*refs, arrive.at[j])
        for j, refs in enumerate(zip(column_tiles(own, 512), column_tiles(here, 512)))
    ]
    outward = [
        pltpu.make_async_copy(*refs, leave.at[j])
        for j, refs in enumerate(zip(column_tiles(here, 512), column_tiles(out, 512)))
    ]
    for copy in inward:
        copy.start()
    for j, copy in enumerate(inward):
        at = slice(j * 512, (j + 1) * 512)
        came = dot(pick_t[...], returned[:, at])
        copy.wait()
        here[:, at] += came
        outward[j].start()
    for copy in outward:
        copy.wait()


def product_kernel(flow, own, far, grad, grad_far, send_out, keep_out):
    _, line = core_and_line()
    mine = (place(1), line)[flow]
    width = keep_out.shape[2]
    for k, which in enumerate((1 - mine, mine)):
        near = (2 * line + which, 2 * which + place(1))[flow]
        total = dot(own[near], grad[...], contract_rows)
        total += dot(far[which], grad_far[...], contract_rows)
        keep_out[k] = total[:, :width]
        send_out[k] = total[:, width:].astype(jnp.bfloat16)


def cores_kernel(keep, got, send_out, keep_out):
    send_out[...] = (keep[0] + got[0].astype(jnp.float32)).astype(jnp.bfloat16)
    keep_out[...] = keep[1] + got[1].astype(jnp.float32)


def split_kernel(bit, keep, got, send_out, keep_out):
    rows = keep_out.shape[0]
    mine = place(bit)
    for which, out in ((1 - mine, send_out), (mine, keep_out)):
        at = pl.ds(pl.multiple_of(which * rows, rows), rows)
        out[...] = (keep[at] + got[at].astype(jnp.float32)).astype(out.dtype)


def add_kernel(keep, got, out):
    out[...] = (keep[...].astype(jnp.float32) + got[...].astype(jnp.float32)).astype(out.dtype)


def join_kernel(bit, own, got, out):
    rows = own.shape[0]
    mine = place(bit)
    out[pl.ds(pl.multiple_of(mine * rows, rows), rows)] = own[...]
    out[pl.ds(pl.multiple_of((1 - mine) * rows, rows), rows)] = got[...]


def stack_kernel(own, got, out):
    out[0] = own[...]
    out[1] = got[...]


def sort_kernel(bit, own_first, got_first, own_second, got_second, send_out, keep_out):
    core, _ = core_and_line()
    pair, mine = place(1), place(bit)
    rows, width = own_first.shape
    part = rows // 2
    for block, out in ((1 - core, send_out), (core, keep_out)):
        own_block = block == pair

        @pl.when(own_block)
        def _():
            out[:, :width] = own_first[...]

        @pl.when(jnp.logical_not(own_block))
        def _():
            out[:, :width] = got_first[...]

        which = jnp.where(own_block, 0, 1)
        out[pl.ds(pl.multiple_of(mine * part, part), part), width:] = own_second[which]
        out[pl.ds(pl.multiple_of((1 - mine) * part, part), part), width:] = got_second[which]


def place_kernel(own, *refs):
    parts, (out, wide, leave) = refs[:splits], refs[-3:]
    core, _ = core_and_line()
    half = core if own else 1 - core
    rows, piece = parts[0].shape[0], sum(chunk_widths)
    height = rows // 2
    copies = []
    for j in range(2):
        here = pl.ds(j * height, height)
        for flow in (0, 1):
            for chunk, width in enumerate(chunk_widths):
                first = flow * piece + sum(chunk_widths[:chunk])
                at = pl.ds(first, width)
                wide[here, at] = parts[chunk][here, pl.ds(flow * width, width)].astype(jnp.float32)
                column = pl.multiple_of(half * 2 * piece + first, 128)
                target = out.at[here, pl.ds(column, width)]
                copies.append(pltpu.make_async_copy(wide.at[here, at], target, leave.at[len(copies)]))
                copies[-1].start()
    for copy in copies:
        copy.wait()


kernel_waits = {(1, 1): [(0, 0, 0), (0, 1, 0)], (1, 3): [(3, 0, 0), (3, 1, 0)], (1, 2): [(2, 0, 0), (2, 1, 0)]}
swap_waits = {}


class WeightGradient:
    def __init__(self, mixed, to_share):
        self.mixed, self.far = mixed, list(to_share)
        _, self.rows, self.piece = mixed.shape
        self.ended, self.summed = {}, {}

    def over(self, flow, value):
        return swap(value, "sub", 2) if flow == 0 else swap(value, "dom", 1)

    def share(self, flow, start):
        self.far[flow] = self.over(flow, after(self.far[flow], start))

    def ordered(self, step, flow, chunk, value, move):
        keys = swap_waits.get((chunk, step), ())
        value = after(value, *(self.ended[key] for key in keys if key in self.ended))
        value = move(value)
        self.ended[step, flow, chunk] = value
        return value

    def gate(self, step, chunk, value, flow):
        return after(value, *(self.ended[key] for key in kernel_waits.get((chunk, step), ()) if key in self.ended))

    def spread(self, flow, chunk):
        near = self.near[flow * splits + chunk]
        self.grad_far[flow, chunk] = self.ordered(0, flow, chunk, near, functools.partial(self.over, flow))

    def product(self, flow, chunk, gate):
        piece, rows = self.piece, self.rows
        far = self.grad_far[flow, chunk]
        width = far.shape[1] // 2
        send, keep = call(
            functools.partial(product_kernel, flow),
            [struct((2, piece, width), jnp.bfloat16), struct((2, piece, width))],
            16 * rows * piece * width,
            self.mixed,
            self.far[flow],
            self.near[flow * splits + chunk],
            after(far, gate) if gate is not None else far,
        )
        send, keep = call(
            cores_kernel,
            [struct((piece, width), jnp.bfloat16), struct((piece, width))],
            piece * width,
            keep,
            swap(send, "sub", 1),
        )
        self.summed.setdefault(chunk, []).append(send)
        return send, keep

    def chunk_steps(self, chunk, gate):
        bits = [1 << k for k in range(lax.axis_size("dom").bit_length() - 1)]
        rest = bits[1:]
        flows = (0, 1)
        step = 0

        def move(flow, value, axis, bit):
            return self.ordered(step, flow, chunk, value, lambda v: swap(v, axis, bit))

        for flow in flows:
            self.spread(flow, chunk)
        yield
        step += 1
        sends, parts = zip(*[self.product(flow, chunk, gate) for flow in flows])
        links = (("dom", 1), ("sub", 2))
        gots = [move(flow, sends[flow], *links[flow]) for flow in flows]
        parts = list(parts)
        yield
        for bit in rest[:-1]:
            step += 1
            for flow in flows:
                rows, width = parts[flow].shape
                send, parts[flow] = call(
                    functools.partial(split_kernel, bit),
                    [struct((rows // 2, width), jnp.bfloat16), struct((rows // 2, width))],
                    rows * width,
                    self.gate(step, chunk, parts[flow], flow),
                    gots[flow],
                )
                gots[flow] = move(flow, send, "dom", bit)
            yield
        step += 1
        for flow in flows:
            shape = struct(parts[flow].shape, jnp.bfloat16)
            kept = self.gate(step, chunk, parts[flow], flow)
            parts[flow] = call(add_kernel, shape, 1000, kept, gots[flow])
            gots[flow] = move(flow, parts[flow], "dom", rest[-1])
        yield
        for flow in flows:
            shape = struct(parts[flow].shape, jnp.bfloat16)
            kept = self.gate(step + 1, chunk, parts[flow], flow)
            parts[flow] = call(add_kernel, shape, 1000, kept, gots[flow])

        def join(part, flow, bit):
            rows, width = part.shape
            return call(
                functools.partial(join_kernel, bit),
                struct((2 * rows, width), jnp.bfloat16),
                rows * width,
                part,
                move(flow, part, "dom", bit),
            )

        first, second = parts
        for bit in reversed(rest[1:-1]):
            step += 1
            first, second = join(first, 0, bit), join(second, 1, bit)
            yield
        step += 1
        first = join(first, 0, rest[0])
        second = call(
            stack_kernel,
            struct((2,) + second.shape, jnp.bfloat16),
            second.size,
            second,
            move(1, second, "dom", 1),
        )
        yield
        step += 1
        first_got = move(0, first, "dom", 1)
        second_got = move(1, second, "dom", rest[0])
        yield
        if self.features is None:
            self.features = self.features_out(second)
        rows, width = first.shape
        send, keep = call(
            functools.partial(sort_kernel, rest[0]),
            [struct((rows, 2 * width), jnp.bfloat16)] * 2,
            rows * width,
            after(first, self.features),
            first_got,
            second,
            second_got,
        )
        other = swap(send, "sub", 1)
        self.results[chunk] = keep, other

    def finish(self, gate, features_out, send_back):
        self.results, self.features_out, self.features, self.out = {}, features_out, None, None
        chunks = [self.chunk_steps(chunk, gate) for chunk in range(splits)]
        tick, running = 0, set(range(splits))
        while running:
            for chunk in sorted(running):
                if tick >= chunk * lag:
                    try:
                        next(chunks[chunk])
                    except StopIteration:
                        running.discard(chunk)
            if tick == 1:
                send_back(self.ended[0, 0, 0], self.ended[0, 1, 0])
            tick += 1
        out = None
        for own in (True, False):
            out = self.place(own, [self.results[chunk][1 - own] for chunk in range(splits)], out)
        return out, self.features

    def place(self, own, parts, out):
        rows, width = parts[0].shape[0], 2 * sum(chunk_widths)
        into = {} if out is None else dict(far=(splits,), alias={splits: 0})
        return call(
            functools.partial(place_kernel, own),
            struct((rows, 2 * width)),
            1,
            *parts,
            *([] if out is None else [out]),
            far_out=(0,),
            scratch=[
                pltpu.VMEM((rows, width), jnp.float32),
                pltpu.SemaphoreType.DMA((4 * splits,)),
            ],
            **into,
        )


def on_device(
    features, weight, bn_gain, bn_shift, cotangent, neighbours, degrees, send_rows, valid_nodes
):
    rows, width = features.shape
    halo = send_rows.size
    devices = lax.axis_size("dom") * lax.axis_size("sub")
    piece = width // 4

    def to_all(value):
        value = value.reshape(devices, halo // devices, width)
        return lax.all_to_all(value, both_axes, 0, 0, tiled=True).reshape(halo, width)

    routes = send_rows.reshape(devices, halo // devices)
    outgoing = call(
        pick_kernel,
        struct((halo, width), jnp.bfloat16),
        2 * halo * rows * width,
        routes,
        features,
        far=(0, 1),
        far_out=(0,),
        scratch=[
            pltpu.VMEM(routes.shape, jnp.int32),
            pltpu.VMEM((rows, width), jnp.bfloat16),
            pltpu.VMEM((halo, width), jnp.bfloat16),
            pltpu.SemaphoreType.DMA,
            pltpu.SemaphoreType.DMA((width // 1024,)),
            pltpu.SemaphoreType.DMA((width // 1024,)),
        ],
        vmem=6 + (halo * width >> 19),
    )
    arrived = to_all(outgoing)
    gain, shift = bn_gain[None, :], bn_shift[None, :]
    counts_t, scale, mask, pick_t = call(
        counts_kernel,
        [
            struct((rows + halo, rows), jnp.bfloat16),
            struct((rows, 1)),
            struct((rows, 1)),
            struct((rows, halo), jnp.bfloat16),
        ],
        3 * neighbours.size * (rows + halo),
        neighbours.T,
        degrees[None, :],
        valid_nodes[None, :],
        routes,
    )

    share = struct((2, rows, piece), jnp.bfloat16)
    mixed, *to_share, linear, stats, weight_here = call(
        linear_kernel,
        [
            struct((4, rows, piece), jnp.bfloat16),
            share,
            share,
            struct((rows, width)),
            struct((3, width)),
            struct(weight.shape, jnp.bfloat16),
        ],
        2 * rows * width * (width + rows + halo),
        counts_t,
        features,
        arrived,
        scale,
        mask,
        weight,
        far=(5,),
        near_out=(5,),
        scratch=[pltpu.SemaphoreType.DMA((width // 512,))],
    )

    product = WeightGradient(mixed, to_share)
    stats, merged = merge_statistics(stats)
    for flow in (0, 1):
        product.share(flow, merged[flow])

    active, slope, sums = call(
        gelu_kernel,
        [struct((rows, width), jnp.bfloat16), struct((rows, width)), struct((2, width))],
        40 * rows * width,
        linear,
        stats,
        gain,
        shift,
        cotangent,
        mask,
        far_out=(0,),
        scratch=[pltpu.VMEM((rows, width), jnp.bfloat16), pltpu.SemaphoreType.DMA],
    )
    sums, product.far[0] = lax.optimization_barrier((sums, product.far[0]))
    sums, product.far[1] = sum_over_all(sums, product.far[1])

    grad, grad_gain, grad_shift, *near = call(
        grad_kernel,
        [struct((4, rows, piece), jnp.bfloat16), struct((1, width)), struct((1, width))]
        + [struct((rows, 2 * wide), jnp.bfloat16) for wide in chunk_widths] * 2,
        10 * rows * width,
        linear,
        stats,
        sums,
        gain,
        slope,
        mask,
    )
    product.near, product.grad_far = near, {}
    own_grad, halo_grad = call(
        back_kernel,
        [struct((rows, width)), struct((halo, width), jnp.bfloat16)],
        2 * rows * width * (width + rows + halo),
        grad,
        weight_here,
        counts_t,
        scale,
        far_out=(0, 1),
        scratch=[
            pltpu.VMEM((rows, width), jnp.float32),
            pltpu.VMEM((halo, width), jnp.bfloat16),
            pltpu.SemaphoreType.DMA((2 * width // 1024,)),
        ],
        vmem=6 + (halo * width >> 19),
    )

    def send_back(*start):
        product.returned = to_all(after(halo_grad, *start))

    def features_out(start):
        return call(
            last_kernel,
            struct((rows, width)),
            2 * rows * width * halo,
            own_grad,
            pick_t,
            after(product.returned, start),
            far=(0,),
            far_out=(0,),
            scratch=[
                pltpu.VMEM((rows, width), jnp.float32),
                pltpu.SemaphoreType.DMA((width // 512,)),
                pltpu.SemaphoreType.DMA((width // 512,)),
            ],
        )

    grad_weight, grad_features = product.finish(halo_grad, features_out, send_back)
    return (active, grad_features, grad_weight, grad_gain[0], grad_shift[0])


def solution(mesh):
    return jax.shard_map(
        on_device,
        mesh=mesh,
        in_specs=(
            P(("dom", "sub"), None),
            P(),
            P(),
            P(),
            P(("dom", "sub"), None),
            P(("dom", "sub"), None),
            P(("dom", "sub")),
            P(("dom", "sub"), None, None, None),
            P(("dom", "sub")),
        ),
        out_specs=(P(("dom", "sub"), None), P(("dom", "sub"), None), P("sub", None), P(), P()),
        check_vma=False,
    )
```

```python
import functools
import math

import jax
import jax.numpy as jnp
from jax import lax
from jax.experimental import pallas as pl
from jax.experimental.pallas import tpu as pltpu
from jax.sharding import PartitionSpec as P

epsilon = 1e-05
chunk_widths = (256, 256)
splits = len(chunk_widths)
lag = 1
both_axes = ("dom", "sub")
contract_rows = (((0,), (0,)), ((), ()))
contract_columns = (((1,), (1,)), ((), ()))


def swap(value, axis, offset):
    size = lax.axis_size(axis)
    return lax.ppermute(value, axis, [(i, i ^ offset) for i in range(size)])


def tree_sum(terms):
    while len(terms) > 1:
        terms = [terms[i] + terms[i + 1] for i in range(0, len(terms), 2)]
    return terms[0]


def exchange_steps():
    steps = []
    for axis in ("sub", "dom"):
        size, low = lax.axis_size(axis), 1
        odd = (size.bit_length() - 1) % 2
        while low < size:
            width = 2 if odd else 4
            odd = 0
            steps.append((axis, [low * k for k in range(1, width)]))
            low *= width
    return steps


def sum_over_all(value, other):
    for step, (axis, offsets) in enumerate(exchange_steps()):
        if step == 1:
            value, other = lax.optimization_barrier((value, other))
        value = tree_sum([value] + [swap(value, axis, offset) for offset in offsets])
    return value, other


def merge_kernel(*refs):
    *parts, out = refs
    parts = [(p[0:1], p[1:2], p[2:3]) for p in parts]
    count = tree_sum([p[0] for p in parts])
    total = tree_sum([p[1] for p in parts])
    mean = total / jnp.maximum(count, 1.0)
    out[0:1] = count
    out[1:2] = total
    out[2:3] = tree_sum([p[2] + p[0] * jnp.square(p[1] / jnp.maximum(p[0], 1.0) - mean) for p in parts])


def merge_statistics(packed):
    steps = []
    for axis, offsets in exchange_steps():
        parts = [packed] + [swap(packed, axis, offset) for offset in offsets]
        packed = call(merge_kernel, struct(packed.shape), 30 * packed.size, *parts)
        steps.append(packed)
    return packed, steps


def after(value, *others):
    return lax.optimization_barrier((value,) + others)[0]


def place(bit):
    return (lax.axis_index("dom") // bit) % 2


def core_and_line():
    sub = lax.axis_index("sub")
    return sub % 2, sub // 2


def bytes_of(shapes):
    return sum(math.prod(s.shape) * s.dtype.itemsize for s in shapes)


def call(
    kernel, out_shape, flops, *operands, far=(), far_out=(), near_out=(), scratch=(), vmem=6, alias=None
):
    several = isinstance(out_shape, list)
    outs = out_shape if several else [out_shape]

    def specs(count, away):
        return [
            pl.BlockSpec(memory_space=pltpu.HBM if i in away else pltpu.VMEM) for i in range(count)
        ]

    out_specs = specs(len(outs), far_out)
    results = list(outs)
    for i in far_out:
        results[i] = pltpu.HBM(outs[i].shape, outs[i].dtype)
    for i in near_out:
        results[i] = pltpu.VMEM(outs[i].shape, outs[i].dtype)
    operands = [
        pltpu.with_memory_space_constraint(x, pltpu.HBM) if i in far else x
        for i, x in enumerate(operands)
    ]
    return pl.pallas_call(
        kernel,
        in_specs=specs(len(operands), far),
        out_specs=out_specs if several else out_specs[0],
        out_shape=results if several else results[0],
        scratch_shapes=scratch,
        input_output_aliases=alias or {},
        compiler_params=pltpu.CompilerParams(vmem_limit_bytes=vmem * 2**20),
        cost_estimate=pl.CostEstimate(
            flops=1, bytes_accessed=1, transcendentals=0
        ),
    )(*operands)


def struct(shape, dtype=jnp.float32):
    return jax.ShapeDtypeStruct(shape, dtype)


def dot(a, b, dims=(((1,), (0,)), ((), ()))):
    return lax.dot_general(a, b, dims, preferred_element_type=jnp.float32)


def tiles(length, width, body):
    def step(i, carry):
        body(i, pl.ds(pl.multiple_of(i * width, width), width))
        return carry

    lax.fori_loop(0, length // width, step, 0)


def column_tiles(array, width):
    return [array.at[:, pl.ds(j * width, width)] for j in range(array.shape[1] // width)]


def picked(routes, rows):
    devices, slots = routes.shape
    halo = devices * slots
    slot_of = lax.broadcasted_iota(jnp.int32, (slots, halo), 1) % slots
    spread = (slot_of == lax.broadcasted_iota(jnp.int32, (slots, halo), 0)).astype(jnp.bfloat16)
    by_device = dot(routes[...].astype(jnp.float32).astype(jnp.bfloat16), spread)
    device_of = lax.broadcasted_iota(jnp.int32, (devices, halo), 1) // slots
    here = device_of == lax.broadcasted_iota(jnp.int32, (devices, halo), 0)
    wanted = jnp.sum(jnp.where(here, by_device, 0.0), 0, keepdims=True).astype(jnp.int32)
    return (wanted == lax.broadcasted_iota(jnp.int32, (rows, halo), 0)).astype(jnp.bfloat16)


def pick_kernel(send_rows, features, out, routes, features_here, out_here, reach, arrive, leave):
    inward = [
        pltpu.make_async_copy(*refs, arrive.at[j])
        for j, refs in enumerate(
            zip(column_tiles(features, 1024), column_tiles(features_here, 1024))
        )
    ]
    outward = [
        pltpu.make_async_copy(*refs, leave.at[j])
        for j, refs in enumerate(zip(column_tiles(out_here, 1024), column_tiles(out, 1024)))
    ]
    rows_in = pltpu.make_async_copy(send_rows, routes, reach)
    rows_in.start()
    for copy in inward:
        copy.start()
    rows_in.wait()
    pick = picked(routes, features.shape[0])
    for j, copy in enumerate(inward):
        copy.wait()
        at = slice(j * 1024, (j + 1) * 1024)
        out_here[:, at] = dot(pick, features_here[:, at], contract_rows).astype(jnp.bfloat16)
        outward[j].start()
    for copy in outward:
        copy.wait()


def counts_kernel(
    neighbours, degrees, valid, routes, counts_out, scale_out, mask_out, pick_out
):
    slots, rows = neighbours.shape
    table = counts_out.shape[0]
    pick_out[...] = picked(routes, rows)
    step = 64

    def lanes_to_rows(value):
        return jnp.transpose(jnp.broadcast_to(value, (128, rows)))[:, :1]

    scale_out[...] = lanes_to_rows(1.0 / (degrees[...].astype(jnp.float32) + 1.0))
    mask_out[...] = lanes_to_rows(valid[...].astype(jnp.float32))
    own = lax.broadcasted_iota(jnp.int32, (1, rows), 1)

    def body(i, carry):
        at = pl.ds(pl.multiple_of(i * step, step), step)
        entry = i * step + lax.broadcasted_iota(jnp.int32, (step, rows), 0)
        total = jnp.where(entry == own, 2.0, 0.0)
        for k in range(slots):
            used = jnp.where(degrees[...] > k, neighbours[k : k + 1], -1)
            total += jnp.where(entry == used, 1.0, 0.0)
        counts_out[at] = total.astype(jnp.bfloat16)
        return carry

    lax.fori_loop(0, table // step, body, 0)


def linear_kernel(
    counts_t,
    features,
    arrived,
    scale,
    mask,
    weight,
    mixed_out,
    line_out,
    pair_out,
    linear_out,
    stats_out,
    weight_here,
    arrive,
):
    tile = 512
    copies = [
        pltpu.make_async_copy(*refs, arrive.at[j])
        for j, refs in enumerate(zip(column_tiles(weight, tile), column_tiles(weight_here, tile)))
    ]
    for copy in copies:
        copy.start()
    rows, width = features.shape
    pieces, _, piece = mixed_out.shape
    for j in range(pieces):
        part = slice(j * piece, (j + 1) * piece)
        summed = dot(counts_t[:rows], features[:, part], contract_rows)
        summed += dot(counts_t[rows:], arrived[:, part], contract_rows)
        mixed_out[j] = (summed * scale[...]).astype(jnp.bfloat16)
    _, line = core_and_line()
    pair = place(1)
    for j in range(2):
        line_out[j] = mixed_out[2 * (1 - line) + j]
        pair_out[j] = mixed_out[2 * j + (1 - pair)]
    count = jnp.sum(mask[...])
    for i, copy in enumerate(copies):
        copy.wait()
        at = slice(i * tile, (i + 1) * tile)
        linear = dot(mixed_out[0], weight_here[:piece, at])
        for j in range(1, pieces):
            linear += dot(mixed_out[j], weight_here[j * piece : (j + 1) * piece, at])
        linear_out[:, at] = linear
        total = jnp.sum(mask[...] * linear, 0, keepdims=True)
        off = linear - total / jnp.maximum(count, 1.0)
        stats_out[0:1, at] = jnp.full_like(total, count)
        stats_out[1:2, at] = total
        stats_out[2:3, at] = jnp.sum(mask[...] * off * off, 0, keepdims=True)


def column_terms(stats):
    count = stats[0:1]
    return stats[1:2] / count, lax.rsqrt(stats[2:3] / count + epsilon), count


def gelu_kernel(
    linear, stats, gain, shift, cotangent, mask, active, slope_out, sums_out, active_here, leave
):
    rows, width = linear.shape
    root, cubic = 0.7978845608028654, 0.044715

    def copy(at):
        return pltpu.make_async_copy(active_here.at[:, at], active.at[:, at], leave)

    def body(i, at):
        mean, inverse, _ = column_terms(stats[:, at])
        first = second = 0.0
        for r in range(0, rows, 64):
            here = slice(r, r + 64)
            normed = (linear[here, at] - mean) * inverse
            value = gain[:, at] * normed + shift[:, at]
            square = value * value
            bent = jnp.tanh(root * value * (1.0 + cubic * square))
            upper = 0.5 * (1.0 + bent)
            active_here[here, at] = (mask[here] * (value * upper)).astype(jnp.bfloat16)
            inner = 0.5 * root * value * (1.0 - bent * bent) * (1.0 + 3.0 * cubic * square)
            slope = mask[here] * cotangent[here, at].astype(jnp.float32) * (upper + inner)
            slope_out[here, at] = slope
            first = first + jnp.sum(slope * normed, 0, keepdims=True)
            second = second + jnp.sum(slope, 0, keepdims=True)
        sums_out[0:1, at] = first
        sums_out[1:2, at] = second
        copy(at).start()

    tiles(width, 256, body)
    pltpu.make_async_copy(active_here, active, leave).wait()


def grad_kernel(linear, stats, sums, gain, slope, mask, grad_out, gain_out, shift_out, *near):
    rows, width = linear.shape
    pieces, _, piece = grad_out.shape
    gain_out[...] = sums[0:1]
    shift_out[...] = sums[1:2]

    def body(i, at):
        mean, inverse, count = column_terms(stats[:, at])
        factor = gain[:, at] * inverse
        along, offset = sums[0:1, at] / count, sums[1:2, at] / count
        for r in range(0, rows, 32):
            here = slice(r, r + 32)
            normed = (linear[here, at] - mean) * inverse
            grad_out[i, here] = (
                mask[here] * factor * (slope[here, at] - (offset + normed * along))
            ).astype(jnp.bfloat16)

    tiles(width, piece, body)
    core, _ = core_and_line()
    for k, out in enumerate(near):
        flow, chunk = divmod(k, splits)
        part = out.shape[1] // 2
        first = sum(chunk_widths[:chunk])
        at = slice(first, first + part)
        out[:, :part] = grad_out[2 * core + flow, :, at]
        out[:, part:] = grad_out[2 * (1 - core) + flow, :, at]


def back_kernel(grad, weight, counts_t, scale, own, halo, own_here, halo_here, leave):
    pieces, rows, piece = grad.shape
    tile = 1024
    outward = []
    for i in range(weight.shape[0] // tile):
        at = slice(i * tile, (i + 1) * tile)
        total = dot(grad[0], weight[at, :piece], contract_columns)
        for b in range(1, pieces):
            total += dot(grad[b], weight[at, b * piece : (b + 1) * piece], contract_columns)
        weighted = (total * scale[...]).astype(jnp.bfloat16)
        halo_here[:, at] = dot(counts_t[rows:], weighted).astype(jnp.bfloat16)
        own_here[:, at] = dot(counts_t[:rows], weighted)
        for k, refs in enumerate(((halo_here, halo), (own_here, own))):
            source, target = (ref.at[:, pl.ds(i * tile, tile)] for ref in refs)
            outward.append(pltpu.make_async_copy(source, target, leave.at[2 * i + k]))
            outward[-1].start()
    for copy in outward:
        copy.wait()


def last_kernel(own, pick_t, returned, out, here, arrive, leave):
    inward = [
        pltpu.make_async_copy(*refs, arrive.at[j])
        for j, refs in enumerate(zip(column_tiles(own, 512), column_tiles(here, 512)))
    ]
    outward = [
        pltpu.make_async_copy(*refs, leave.at[j])
        for j, refs in enumerate(zip(column_tiles(here, 512), column_tiles(out, 512)))
    ]
    for copy in inward:
        copy.start()
    for j, copy in enumerate(inward):
        at = slice(j * 512, (j + 1) * 512)
        came = dot(pick_t[...], returned[:, at])
        copy.wait()
        here[:, at] += came
        outward[j].start()
    for copy in outward:
        copy.wait()


def product_kernel(flow, own, far, grad, grad_far, send_out, keep_out):
    _, line = core_and_line()
    mine = (place(1), line)[flow]
    width = keep_out.shape[2]
    for k, which in enumerate((1 - mine, mine)):
        near = (2 * line + which, 2 * which + place(1))[flow]
        total = dot(own[near], grad[...], contract_rows)
        total += dot(far[which], grad_far[...], contract_rows)
        keep_out[k] = total[:, :width]
        send_out[k] = total[:, width:].astype(jnp.bfloat16)


def cores_kernel(keep, got, send_out, keep_out):
    send_out[...] = (keep[0] + got[0].astype(jnp.float32)).astype(jnp.bfloat16)
    keep_out[...] = keep[1] + got[1].astype(jnp.float32)


def split_kernel(bit, keep, got, send_out, keep_out):
    rows = keep_out.shape[0]
    mine = place(bit)
    for which, out in ((1 - mine, send_out), (mine, keep_out)):
        at = pl.ds(pl.multiple_of(which * rows, rows), rows)
        out[...] = (keep[at] + got[at].astype(jnp.float32)).astype(out.dtype)


def add_kernel(keep, got, out):
    out[...] = (keep[...].astype(jnp.float32) + got[...].astype(jnp.float32)).astype(out.dtype)


def join_kernel(bit, own, got, out):
    rows = own.shape[0]
    mine = place(bit)
    out[pl.ds(pl.multiple_of(mine * rows, rows), rows)] = own[...]
    out[pl.ds(pl.multiple_of((1 - mine) * rows, rows), rows)] = got[...]


def stack_kernel(own, got, out):
    out[0] = own[...]
    out[1] = got[...]


def sort_kernel(bit, own_first, got_first, own_second, got_second, send_out, keep_out):
    core, _ = core_and_line()
    pair, mine = place(1), place(bit)
    rows, width = own_first.shape
    part = rows // 2
    for block, out in ((1 - core, send_out), (core, keep_out)):
        own_block = block == pair

        @pl.when(own_block)
        def _():
            out[:, :width] = own_first[...]

        @pl.when(jnp.logical_not(own_block))
        def _():
            out[:, :width] = got_first[...]

        which = jnp.where(own_block, 0, 1)
        out[pl.ds(pl.multiple_of(mine * part, part), part), width:] = own_second[which]
        out[pl.ds(pl.multiple_of((1 - mine) * part, part), part), width:] = got_second[which]


def place_kernel(own, *refs):
    parts, (out, wide, leave) = refs[:splits], refs[-3:]
    core, _ = core_and_line()
    half = core if own else 1 - core
    rows, piece = parts[0].shape[0], sum(chunk_widths)
    height = rows // 2
    copies = []
    for j in range(2):
        here = pl.ds(j * height, height)
        for flow in (0, 1):
            for chunk, width in enumerate(chunk_widths):
                first = flow * piece + sum(chunk_widths[:chunk])
                at = pl.ds(first, width)
                wide[here, at] = parts[chunk][here, pl.ds(flow * width, width)].astype(jnp.float32)
                column = pl.multiple_of(half * 2 * piece + first, 128)
                target = out.at[here, pl.ds(column, width)]
                copies.append(pltpu.make_async_copy(wide.at[here, at], target, leave.at[len(copies)]))
                copies[-1].start()
    for copy in copies:
        copy.wait()


kernel_waits = {(1, 1): [(0, 0, 0), (0, 1, 0)], (1, 3): [(3, 0, 0), (3, 1, 0)], (1, 2): [(2, 0, 0), (2, 1, 0)]}
swap_waits = {(0, 2): [(0, 1, 1)]}


class WeightGradient:
    def __init__(self, mixed, to_share):
        self.mixed, self.far = mixed, list(to_share)
        _, self.rows, self.piece = mixed.shape
        self.ended, self.summed = {}, {}

    def over(self, flow, value):
        return swap(value, "sub", 2) if flow == 0 else swap(value, "dom", 1)

    def share(self, flow, start):
        self.far[flow] = self.over(flow, after(self.far[flow], start))

    def ordered(self, step, flow, chunk, value, move):
        keys = swap_waits.get((chunk, step), ())
        value = after(value, *(self.ended[key] for key in keys if key in self.ended))
        value = move(value)
        self.ended[step, flow, chunk] = value
        return value

    def gate(self, step, chunk, value, flow):
        return after(value, *(self.ended[key] for key in kernel_waits.get((chunk, step), ()) if key in self.ended))

    def spread(self, flow, chunk):
        near = self.near[flow * splits + chunk]
        self.grad_far[flow, chunk] = self.ordered(0, flow, chunk, near, functools.partial(self.over, flow))

    def product(self, flow, chunk, gate):
        piece, rows = self.piece, self.rows
        far = self.grad_far[flow, chunk]
        width = far.shape[1] // 2
        send, keep = call(
            functools.partial(product_kernel, flow),
            [struct((2, piece, width), jnp.bfloat16), struct((2, piece, width))],
            16 * rows * piece * width,
            self.mixed,
            self.far[flow],
            self.near[flow * splits + chunk],
            after(far, gate) if gate is not None else far,
        )
        send, keep = call(
            cores_kernel,
            [struct((piece, width), jnp.bfloat16), struct((piece, width))],
            piece * width,
            keep,
            swap(send, "sub", 1),
        )
        self.summed.setdefault(chunk, []).append(send)
        return send, keep

    def chunk_steps(self, chunk, gate):
        bits = [1 << k for k in range(lax.axis_size("dom").bit_length() - 1)]
        rest = bits[1:]
        flows = (0, 1)
        step = 0

        def move(flow, value, axis, bit):
            return self.ordered(step, flow, chunk, value, lambda v: swap(v, axis, bit))

        for flow in flows:
            self.spread(flow, chunk)
        yield
        step += 1
        sends, parts = zip(*[self.product(flow, chunk, gate) for flow in flows])
        links = (("dom", 1), ("sub", 2))
        gots = [move(flow, sends[flow], *links[flow]) for flow in flows]
        parts = list(parts)
        yield
        for bit in rest[:-1]:
            step += 1
            for flow in flows:
                rows, width = parts[flow].shape
                send, parts[flow] = call(
                    functools.partial(split_kernel, bit),
                    [struct((rows // 2, width), jnp.bfloat16), struct((rows // 2, width))],
                    rows * width,
                    self.gate(step, chunk, parts[flow], flow),
                    gots[flow],
                )
                gots[flow] = move(flow, send, "dom", bit)
            yield
        step += 1
        for flow in flows:
            shape = struct(parts[flow].shape, jnp.bfloat16)
            kept = self.gate(step, chunk, parts[flow], flow)
            parts[flow] = call(add_kernel, shape, 1000, kept, gots[flow])
            gots[flow] = move(flow, parts[flow], "dom", rest[-1])
        yield
        for flow in flows:
            shape = struct(parts[flow].shape, jnp.bfloat16)
            kept = self.gate(step + 1, chunk, parts[flow], flow)
            parts[flow] = call(add_kernel, shape, 1000, kept, gots[flow])

        def join(part, flow, bit):
            rows, width = part.shape
            return call(
                functools.partial(join_kernel, bit),
                struct((2 * rows, width), jnp.bfloat16),
                rows * width,
                part,
                move(flow, part, "dom", bit),
            )

        first, second = parts
        for bit in reversed(rest[1:-1]):
            step += 1
            first, second = join(first, 0, bit), join(second, 1, bit)
            yield
        step += 1
        first = join(first, 0, rest[0])
        second = call(
            stack_kernel,
            struct((2,) + second.shape, jnp.bfloat16),
            second.size,
            second,
            move(1, second, "dom", 1),
        )
        yield
        step += 1
        first_got = move(0, first, "dom", 1)
        second_got = move(1, second, "dom", rest[0])
        yield
        if self.features is None:
            self.features = self.features_out(second)
        rows, width = first.shape
        send, keep = call(
            functools.partial(sort_kernel, rest[0]),
            [struct((rows, 2 * width), jnp.bfloat16)] * 2,
            rows * width,
            after(first, self.features),
            first_got,
            second,
            second_got,
        )
        other = swap(send, "sub", 1)
        self.results[chunk] = keep, other

    def finish(self, gate, features_out, send_back):
        self.results, self.features_out, self.features, self.out = {}, features_out, None, None
        chunks = [self.chunk_steps(chunk, gate) for chunk in range(splits)]
        tick, running = 0, set(range(splits))
        while running:
            for chunk in sorted(running):
                if tick >= chunk * lag:
                    try:
                        next(chunks[chunk])
                    except StopIteration:
                        running.discard(chunk)
            if tick == 1:
                send_back(self.ended[0, 0, 0], self.ended[0, 1, 0])
            tick += 1
        out = None
        for own in (True, False):
            out = self.place(own, [self.results[chunk][1 - own] for chunk in range(splits)], out)
        return out, self.features

    def place(self, own, parts, out):
        rows, width = parts[0].shape[0], 2 * sum(chunk_widths)
        into = {} if out is None else dict(far=(splits,), alias={splits: 0})
        return call(
            functools.partial(place_kernel, own),
            struct((rows, 2 * width)),
            1,
            *parts,
            *([] if out is None else [out]),
            far_out=(0,),
            scratch=[
                pltpu.VMEM((rows, width), jnp.float32),
                pltpu.SemaphoreType.DMA((4 * splits,)),
            ],
            **into,
        )


def on_device(
    features, weight, bn_gain, bn_shift, cotangent, neighbours, degrees, send_rows, valid_nodes
):
    rows, width = features.shape
    halo = send_rows.size
    devices = lax.axis_size("dom") * lax.axis_size("sub")
    piece = width // 4

    def to_all(value):
        value = value.reshape(devices, halo // devices, width)
        return lax.all_to_all(value, both_axes, 0, 0, tiled=True).reshape(halo, width)

    routes = send_rows.reshape(devices, halo // devices)
    outgoing = call(
        pick_kernel,
        struct((halo, width), jnp.bfloat16),
        2 * halo * rows * width,
        routes,
        features,
        far=(0, 1),
        far_out=(0,),
        scratch=[
            pltpu.VMEM(routes.shape, jnp.int32),
            pltpu.VMEM((rows, width), jnp.bfloat16),
            pltpu.VMEM((halo, width), jnp.bfloat16),
            pltpu.SemaphoreType.DMA,
            pltpu.SemaphoreType.DMA((width // 1024,)),
            pltpu.SemaphoreType.DMA((width // 1024,)),
        ],
        vmem=6 + (halo * width >> 19),
    )
    arrived = to_all(outgoing)
    gain, shift = bn_gain[None, :], bn_shift[None, :]
    counts_t, scale, mask, pick_t = call(
        counts_kernel,
        [
            struct((rows + halo, rows), jnp.bfloat16),
            struct((rows, 1)),
            struct((rows, 1)),
            struct((rows, halo), jnp.bfloat16),
        ],
        3 * neighbours.size * (rows + halo),
        neighbours.T,
        degrees[None, :],
        valid_nodes[None, :],
        routes,
    )

    share = struct((2, rows, piece), jnp.bfloat16)
    mixed, *to_share, linear, stats, weight_here = call(
        linear_kernel,
        [
            struct((4, rows, piece), jnp.bfloat16),
            share,
            share,
            struct((rows, width)),
            struct((3, width)),
            struct(weight.shape, jnp.bfloat16),
        ],
        2 * rows * width * (width + rows + halo),
        counts_t,
        features,
        arrived,
        scale,
        mask,
        weight,
        far=(5,),
        near_out=(5,),
        scratch=[pltpu.SemaphoreType.DMA((width // 512,))],
    )

    product = WeightGradient(mixed, to_share)
    stats, merged = merge_statistics(stats)
    for flow in (0, 1):
        product.share(flow, merged[flow])

    active, slope, sums = call(
        gelu_kernel,
        [struct((rows, width), jnp.bfloat16), struct((rows, width)), struct((2, width))],
        40 * rows * width,
        linear,
        stats,
        gain,
        shift,
        cotangent,
        mask,
        far_out=(0,),
        scratch=[pltpu.VMEM((rows, width), jnp.bfloat16), pltpu.SemaphoreType.DMA],
    )
    sums, product.far[0] = lax.optimization_barrier((sums, product.far[0]))
    sums, product.far[1] = sum_over_all(sums, product.far[1])

    grad, grad_gain, grad_shift, *near = call(
        grad_kernel,
        [struct((4, rows, piece), jnp.bfloat16), struct((1, width)), struct((1, width))]
        + [struct((rows, 2 * wide), jnp.bfloat16) for wide in chunk_widths] * 2,
        10 * rows * width,
        linear,
        stats,
        sums,
        gain,
        slope,
        mask,
    )
    product.near, product.grad_far = near, {}
    own_grad, halo_grad = call(
        back_kernel,
        [struct((rows, width)), struct((halo, width), jnp.bfloat16)],
        2 * rows * width * (width + rows + halo),
        grad,
        weight_here,
        counts_t,
        scale,
        far_out=(0, 1),
        scratch=[
            pltpu.VMEM((rows, width), jnp.float32),
            pltpu.VMEM((halo, width), jnp.bfloat16),
            pltpu.SemaphoreType.DMA((2 * width // 1024,)),
        ],
        vmem=6 + (halo * width >> 19),
    )

    def send_back(*start):
        product.returned = to_all(after(halo_grad, *start))

    def features_out(start):
        return call(
            last_kernel,
            struct((rows, width)),
            2 * rows * width * halo,
            own_grad,
            pick_t,
            after(product.returned, start),
            far=(0,),
            far_out=(0,),
            scratch=[
                pltpu.VMEM((rows, width), jnp.float32),
                pltpu.SemaphoreType.DMA((width // 512,)),
                pltpu.SemaphoreType.DMA((width // 512,)),
            ],
        )

    grad_weight, grad_features = product.finish(halo_grad, features_out, send_back)
    return (active, grad_features, grad_weight, grad_gain[0], grad_shift[0])


def solution(mesh):
    return jax.shard_map(
        on_device,
        mesh=mesh,
        in_specs=(
            P(("dom", "sub"), None),
            P(),
            P(),
            P(),
            P(("dom", "sub"), None),
            P(("dom", "sub"), None),
            P(("dom", "sub")),
            P(("dom", "sub"), None, None, None),
            P(("dom", "sub")),
        ),
        out_specs=(P(("dom", "sub"), None), P(("dom", "sub"), None), P("sub", None), P(), P()),
        check_vma=False,
    )
```
